128 devices in a mesh: tile: 32 (over y, z, core), shard: 4 (over x).
Axes of the slice: x: 4, y: 4, z: 4, core: 2. Of those that a mesh axis runs over, the one named last changes fastest.
Arguments:
- gaussians: float32 [59, 1048576], P(None, ('tile', 'shard')), may hold values from -10 to 10, as said below
- camera: float32 [4], replicated, may hold values from -1000 to 1000, as said below
- fetch_index: int32 [128, 8192], P(('tile', 'shard')), may hold values from 0 to 8191, as said below
- tile_ids: int32 [128, 16], P(('tile', 'shard')), may hold values from 0 to 2047, as said below
- tile_lists: int32 [128, 16, 1024], P(('tile', 'shard')), may hold values from 0 to 8191, as said below
- tile_counts: int32 [128, 16], P(('tile', 'shard')), may hold values from 1 to 1024, as said below
- tile_active: int32 [128, 16], P(('tile', 'shard')), may hold values 0 or 1
- target: float32 [3, 2048, 256], P(None, ('tile', 'shard')), may hold values from 0 to 1
Outputs:
- image: float32 [3, 2048, 256], P(None, ('tile', 'shard'))
- gaussian_grads: float32 [59, 1048576], P(None, ('tile', 'shard'))
The draws below stay inside these ranges and needn't reach their ends.
Inputs may be any that keep to these rules, and one draw needn't show every extreme that they name: `fetch_index`: in row d, block s of 64 entries holds distinct indices into owner s's 8192 Gaussians; over all rows every Gaussian of every owner is named exactly once. `tile_ids`: each row is a part of one permutation of the 2048 screen tiles. `tile_lists`: on each device every table position 0 to 8191 appears once among the used entries of its tiles' lists, in order of increasing depth of the Gaussian; unused entries are 0. `tile_counts`: on each device the counts sum to 8192, and one tile has exactly 1024. `gaussians`: depth (row 2) lies between 2 and 8; the quaternion's w (row 6) lies between 1 and 2; each Gaussian projects near the tile that lists it. `camera`: fx and fy near 8 * 64; the principal point near the image centre.
All inputs are finite; a program needn't handle non-finite values. No bound on the sum of `tile_active` on one device may be relied on, other than what follows from the above.
Results may differ from the reference program's by a relative error of at most 0.0003.
Values sent between devices are 32-bit elements; how exact they have to be, the bound alone decides.
No kernel may reach another device: no remote copies, remote signals or barrier semaphores. Data moves between devices by JAX's collectives and lax.ppermute only.
A program may use at most 128 MiB of HBM per device.

```python
import jax
import jax.numpy as jnp
from jax import lax

CAP = 64
TILES_DEV = 16
TILE_SIDE = 16
SPAN = 256
TILES_X = 64
NEED = 8192
G_DEV = 8192
GAUSSIANS = 1048576
LIST = 1024
TILES = 2048
DEVICES = 128


def arrange(key):
    shard_keys = jax.random.split(jax.random.fold_in(key, 101), DEVICES)
    shard_perms = jax.vmap(lambda part_key: jax.random.permutation(part_key, G_DEV))(shard_keys).astype(jnp.int32)
    fetch = shard_perms.reshape(DEVICES, DEVICES, CAP).transpose(1, 0, 2).reshape(DEVICES, NEED)
    rest = NEED - LIST
    base = rest // (TILES_DEV - 1)
    extra = rest % (TILES_DEV - 1)
    swing = jax.random.randint(jax.random.fold_in(key, 102), (DEVICES, (TILES_DEV - 2) // 2), 0, max(base * 5 // 6, 1)).astype(jnp.int32)
    others = jnp.concatenate([base + swing, base - swing, jnp.full((DEVICES, 1), base + extra, jnp.int32)], axis=1)
    counts = jnp.concatenate([jnp.full((DEVICES, 1), LIST, jnp.int32), others], axis=1)
    order_keys = jax.random.split(jax.random.fold_in(key, 103), DEVICES)
    shuffles = jax.vmap(lambda part_key: jax.random.permutation(part_key, TILES_DEV))(order_keys).astype(jnp.int32)
    counts = jnp.take_along_axis(counts, shuffles, axis=1)
    slot_keys = jax.random.split(jax.random.fold_in(key, 104), DEVICES)
    orders = jax.vmap(lambda part_key: jax.random.permutation(part_key, NEED))(slot_keys).astype(jnp.int32)
    starts = jnp.cumsum(counts, axis=1) - counts
    ranks = jnp.arange(LIST, dtype=jnp.int32)
    index = jnp.minimum(starts[:, :, None] + ranks[None, None, :], NEED - 1).reshape(DEVICES, -1)
    lists = jnp.take_along_axis(orders, index, axis=1).reshape(DEVICES, TILES_DEV, LIST)
    lists = jnp.where(ranks[None, None, :] < counts[:, :, None], lists, 0).astype(jnp.int32)
    position = jnp.argsort(orders, axis=1).astype(jnp.int32)
    slot_tile = (jnp.sum((position[:, :, None] >= starts[:, None, :]).astype(jnp.int32), axis=2) - 1).astype(jnp.int32)
    slot_rank = position - jnp.take_along_axis(starts, slot_tile, axis=1)
    screen = jax.random.permutation(jax.random.fold_in(key, 105), TILES).astype(jnp.int32).reshape(DEVICES, TILES_DEV)
    return (fetch, counts, lists, screen, slot_tile, slot_rank, shard_perms)


def lens(key):
    lens_key = jax.random.fold_in(key, 106)
    parts = jax.random.uniform(lens_key, (4,), jnp.float32)
    focal_x = 8.0 * TILES_X * (0.9 + 0.2 * parts[0])
    focal_y = focal_x * (0.95 + 0.1 * parts[1])
    centre_x = 8.0 * TILES_X + 16.0 * parts[2] - 8.0
    centre_y = 8.0 * (TILES // TILES_X) + 16.0 * parts[3] - 8.0
    return jnp.stack([focal_x, focal_y, centre_x, centre_y])


def draw_camera(key, part):
    return lens(key)


def draw_fetch_index(key, part):
    return arrange(key)[0]


def draw_tile_counts(key, part):
    return arrange(key)[1]


def draw_tile_lists(key, part):
    return arrange(key)[2]


def draw_tile_ids(key, part):
    return arrange(key)[3]


def draw_gaussians(key, part):
    fetch, counts, lists, screen, slot_tile, slot_rank, shard_perms = arrange(key)
    camera = lens(key)
    key = jax.random.fold_in(key, 7)
    inverse = jnp.argsort(shard_perms, axis=1).astype(jnp.int32)
    target_dev = inverse // CAP
    slot = jnp.arange(DEVICES, dtype=jnp.int32)[:, None] * CAP + inverse % CAP
    tile_slot = slot_tile[target_dev, slot].reshape(-1)
    rank = slot_rank[target_dev, slot].reshape(-1)
    flat_dev = target_dev.reshape(-1)
    count = counts[flat_dev, tile_slot]
    tile = screen[flat_dev, tile_slot]
    keys = jax.random.split(key, 8)
    total = GAUSSIANS
    jitter = 10.0
    low_sigma, high_sigma = (2.0, 8.0)
    opac = jax.random.uniform(keys[4], (total,), jnp.float32, -6.0, -2.5)
    dc_part = jnp.clip(0.6 * jax.random.normal(keys[5], (3, 1, total), jnp.float32), -2.0, 2.0)
    high_part = jnp.clip(0.25 * jax.random.normal(keys[6], (3, 15, total), jnp.float32), -1.0, 1.0)
    offsets = jax.random.uniform(keys[0], (2, total), jnp.float32, -jitter, jitter)
    pixel_x = (tile % TILES_X * TILE_SIDE).astype(jnp.float32) + 0.5 * TILE_SIDE + offsets[0]
    pixel_y = (tile // TILES_X * TILE_SIDE).astype(jnp.float32) + 0.5 * TILE_SIDE + offsets[1]
    shift = jax.random.uniform(keys[1], (total,), jnp.float32, 0.1, 0.9)
    depth = 2.0 + 6.0 * (rank.astype(jnp.float32) + shift) / count.astype(jnp.float32)
    mean_x = (pixel_x - camera[2]) * depth / camera[0]
    mean_y = (pixel_y - camera[3]) * depth / camera[1]
    sigma_px = jnp.exp(jax.random.uniform(keys[2], (3, total), jnp.float32, jnp.log(low_sigma), jnp.log(high_sigma)))
    log_scale = jnp.log(sigma_px * depth[None, :] / camera[0])
    quat_w = jax.random.uniform(keys[3], (1, total), jnp.float32, 1.0, 2.0)
    quat_rest = jnp.clip(jax.random.normal(keys[7], (3, total), jnp.float32), -2.0, 2.0)
    coeffs = jnp.concatenate([dc_part, high_part], axis=1).reshape(48, total)
    return jnp.concatenate([jnp.stack([mean_x, mean_y, depth]), log_scale, quat_w, quat_rest, opac[None, :], coeffs], axis=0)


def set_ends(result, stream_key, low, top_value):
    extent = result.shape
    place = [jax.random.randint(jax.random.fold_in(stream_key, axis), (), 0, extent[axis]) for axis in range(len(extent))]
    result = result.at[tuple(place)].set(low)
    longest = extent.index(max(extent))
    place[longest] = (place[longest] + 1) % extent[longest]
    return result.at[tuple(place)].set(top_value)


def steps_of(key, dims, cuts, low, largest):
    level = 1.0
    for dim, blocks in cuts:
        steps = jax.random.uniform(jax.random.fold_in(jax.random.fold_in(key, 6), dim), (blocks,), jnp.float32, low / len(cuts), largest / len(cuts))
        level = level * jnp.repeat(jnp.exp(steps), dims[dim] // blocks).reshape((-1,) + (1,) * (len(dims) - 1 - dim))
    return level


def setup_inputs(seed: int = 0) -> dict:
    splits = jax.random.split(jax.random.key(seed), 9)
    return {
        "gaussians": draw_gaussians(jax.random.fold_in(splits[8], 71), 0),
        "camera": draw_camera(jax.random.fold_in(splits[8], 71), 0),
        "fetch_index": draw_fetch_index(jax.random.fold_in(splits[8], 71), 0),
        "tile_ids": draw_tile_ids(jax.random.fold_in(splits[8], 71), 0),
        "tile_lists": draw_tile_lists(jax.random.fold_in(splits[8], 71), 0),
        "tile_counts": draw_tile_counts(jax.random.fold_in(splits[8], 71), 0),
        "tile_active": set_ends((jax.random.randint(splits[6], (DEVICES, TILES_DEV), 0, 8) < 7).astype(jnp.int32), jax.random.fold_in(splits[6], 1), 0, 1),
        "target": jnp.clip(1.0 * jax.random.uniform(splits[7], (3, TILES, TILE_SIDE * TILE_SIDE), jnp.float32) ** steps_of(splits[7], (3, TILES, TILE_SIDE * TILE_SIDE), ((1, 128),), -0.2, 0.2), 0.0, 1.0),
    }


SH_ZERO = 0.28209479177387814
SH_ONE = 0.4886025119029199
SH_TWO = (1.0925484305920792, -1.0925484305920792, 0.31539156525252005, -1.0925484305920792, 0.5462742152960396)
SH_THREE = (-0.5900435899266435, 2.890611442640554, -0.4570457994644658, 0.3731763325901154, -0.4570457994644658, 1.445305721320277, -0.5900435899266435)

def harmonics(dir_x, dir_y, dir_z):
    sq_x, sq_y, sq_z = (dir_x * dir_x, dir_y * dir_y, dir_z * dir_z)
    rows = [SH_ZERO * jnp.ones_like(dir_x), -SH_ONE * dir_y, SH_ONE * dir_z, -SH_ONE * dir_x, SH_TWO[0] * dir_x * dir_y, SH_TWO[1] * dir_y * dir_z, SH_TWO[2] * (2.0 * sq_z - sq_x - sq_y), SH_TWO[3] * dir_x * dir_z, SH_TWO[4] * (sq_x - sq_y), SH_THREE[0] * dir_y * (3.0 * sq_x - sq_y), SH_THREE[1] * dir_x * dir_y * dir_z, SH_THREE[2] * dir_y * (4.0 * sq_z - sq_x - sq_y), SH_THREE[3] * dir_z * (2.0 * sq_z - 3.0 * sq_x - 3.0 * sq_y), SH_THREE[4] * dir_x * (4.0 * sq_z - sq_x - sq_y), SH_THREE[5] * dir_z * (sq_x - sq_y), SH_THREE[6] * dir_x * (sq_x - 3.0 * sq_y)]
    return jnp.stack(rows)

def project(table, camera):
    focal_x, focal_y, centre_x, centre_y = (camera[0], camera[1], camera[2], camera[3])
    mean_x, mean_y, mean_z = (table[0], table[1], table[2])
    spread = jnp.exp(table[3:6])
    quat = table[6:10]
    quat = quat / jnp.sqrt(lax.optimization_barrier(jnp.sum(quat * quat, axis=0)))
    w_part, x_part, y_part, z_part = (quat[0], quat[1], quat[2], quat[3])
    rotate = [[1.0 - 2.0 * (y_part * y_part + z_part * z_part), 2.0 * (x_part * y_part - w_part * z_part), 2.0 * (x_part * z_part + w_part * y_part)], [2.0 * (x_part * y_part + w_part * z_part), 1.0 - 2.0 * (x_part * x_part + z_part * z_part), 2.0 * (y_part * z_part - w_part * x_part)], [2.0 * (x_part * z_part - w_part * y_part), 2.0 * (y_part * z_part + w_part * x_part), 1.0 - 2.0 * (x_part * x_part + y_part * y_part)]]
    scaled = [[rotate[row][col] * spread[col] for col in range(3)] for row in range(3)]
    sigma = [[scaled[row][0] * scaled[col][0] + scaled[row][1] * scaled[col][1] + scaled[row][2] * scaled[col][2] for col in range(3)] for row in range(3)]
    depth_inv = 1.0 / mean_z
    zeros = jnp.zeros_like(mean_z)
    first_row = [focal_x * depth_inv, zeros, -focal_x * mean_x * depth_inv * depth_inv]
    second_row = [zeros, focal_y * depth_inv, -focal_y * mean_y * depth_inv * depth_inv]

    def quadric(left, right):
        total = zeros
        for row in range(3):
            for col in range(3):
                total = total + left[row] * sigma[row][col] * right[col]
        return total
    cov_a = quadric(first_row, first_row) + 0.3
    cov_b = quadric(first_row, second_row)
    cov_c = quadric(second_row, second_row) + 0.3
    determinant = cov_a * cov_c - cov_b * cov_b
    conic_a = cov_c / determinant
    conic_b = -cov_b / determinant
    conic_c = cov_a / determinant
    screen_x = focal_x * mean_x * depth_inv + centre_x
    screen_y = focal_y * mean_y * depth_inv + centre_y
    opacity = jax.nn.sigmoid(table[10])
    radius = jnp.sqrt(mean_x * mean_x + mean_y * mean_y + mean_z * mean_z)
    basis = harmonics(mean_x / radius, mean_y / radius, mean_z / radius)
    coeffs = table[11:59].reshape(3, 16, -1)
    colour = jnp.maximum(lax.optimization_barrier(jnp.sum(coeffs * basis[None], axis=1)) + 0.5, 0.0)
    return jnp.concatenate([jnp.stack([screen_x, screen_y, conic_a, conic_b, conic_c, opacity]), colour], axis=0)

def tile_pass(features, tile, entries, count, live, goal):
    pixels = jnp.arange(TILE_SIDE * TILE_SIDE, dtype=jnp.int32)
    pixel_x = (tile % TILES_X * TILE_SIDE + pixels % TILE_SIDE).astype(jnp.float32) + 0.5
    pixel_y = (tile // TILES_X * TILE_SIDE + pixels // TILE_SIDE).astype(jnp.float32) + 0.5
    length = entries.shape[0]
    blocks = length // SPAN
    picked = features[:, entries].reshape(9, blocks, SPAN).transpose(1, 0, 2)
    keep = ((jnp.arange(length, dtype=jnp.int32) < count) & (live > 0)).astype(jnp.float32).reshape(blocks, SPAN)

    @jax.checkpoint
    def advance(carry, block):
        transmit, colour = carry
        cols, kept = block
        delta_x = pixel_x[None, :] - cols[0][:, None]
        delta_y = pixel_y[None, :] - cols[1][:, None]
        power = -0.5 * (cols[2][:, None] * delta_x * delta_x + cols[4][:, None] * delta_y * delta_y) - cols[3][:, None] * delta_x * delta_y
        alphas = (cols[5] * kept)[:, None] * jnp.exp(power)
        logged = jnp.log1p(-alphas)
        running = jnp.cumsum(logged, axis=0)
        weights = alphas * transmit[None, :] * jnp.exp(running - logged)
        colour = colour + jnp.dot(cols[6:9], weights, precision=lax.Precision.HIGHEST)
        transmit = transmit * jnp.exp(running[-1])
        return ((transmit, colour), None)
    start = (jnp.ones((TILE_SIDE * TILE_SIDE,), jnp.float32), jnp.zeros((3, TILE_SIDE * TILE_SIDE), jnp.float32))
    (transmit, colour), unused = lax.scan(advance, start, (picked, keep))
    residual = colour - goal
    loss = 0.5 * jnp.sum(residual * residual) * (live > 0).astype(jnp.float32)
    return (colour, loss)

def local_step(table, camera, tiles, entries, counts, live, goal):

    def total(values):
        features = project(values, camera)

        def one_tile(pack):
            return tile_pass(features, pack[0], pack[1], pack[2], pack[3], pack[4])
        colours, losses = lax.map(one_tile, (tiles, entries, counts, live, goal.transpose(1, 0, 2)))
        return (jnp.sum(losses), colours)
    loss, pullback, colours = jax.vjp(total, table, has_aux=True)
    grad_table = pullback(jnp.ones_like(loss))[0]
    return (colours.transpose(1, 0, 2), grad_table)

def reference(gaussians, camera, fetch_index, tile_ids, tile_lists, tile_counts, tile_active, target):
    owners = (jnp.arange(NEED, dtype=jnp.int32) // CAP).astype(jnp.int32)

    def visit(device, state):
        image, grads = state
        device = jnp.asarray(device).astype(jnp.int32)
        places = (owners * G_DEV + fetch_index[device]).astype(jnp.int32)
        table = gaussians[:, places]
        first = (device * TILES_DEV).astype(jnp.int32)
        goal = lax.dynamic_slice_in_dim(target, first, TILES_DEV, 1)
        colours, grad_table = local_step(table, camera, tile_ids[device], tile_lists[device], tile_counts[device], tile_active[device], goal)
        image = lax.dynamic_update_slice_in_dim(image, colours, first, 1)
        grads = grads.at[:, places].add(grad_table)
        return (image, grads)
    start = (jnp.zeros((3, TILES, TILE_SIDE * TILE_SIDE), jnp.float32), jnp.zeros_like(gaussians))
    image, grads = lax.fori_loop(0, DEVICES, visit, start)
    return (image, grads)
```

```python
import functools

import jax
import jax.numpy as jnp
from jax import lax
from jax.experimental import pallas as pl
from jax.experimental.pallas import tpu as pltpu
from jax.sharding import PartitionSpec as P

AXES = ("tile", "shard")
SEG = 64
SEGS = 16
GROUP = SEG * SEGS
MAX_GROUPS = 9
STEPS = 16
LOG2E = 1.4426950408889634
LN2 = 0.6931471805599453
FEATS = 9
TRIPLE = (0, 1)
ROWS = 32 * (2 * FEATS + len(TRIPLE))
BACK_ROWS = 32 * 2 * FEATS

SH_ZERO = 0.28209479177387814
SH_ONE = 0.4886025119029199
SH_TWO = (
    1.0925484305920792,
    -1.0925484305920792,
    0.31539156525252005,
    -1.0925484305920792,
    0.5462742152960396,
)
SH_THREE = (
    -0.5900435899266435,
    2.890611442640554,
    -0.4570457994644658,
    0.3731763325901154,
    -0.4570457994644658,
    1.445305721320277,
    -0.5900435899266435,
)


def harmonics(dir_x, dir_y, dir_z):
    sq_x, sq_y, sq_z = (dir_x * dir_x, dir_y * dir_y, dir_z * dir_z)
    return [
        None,
        -SH_ONE * dir_y,
        SH_ONE * dir_z,
        -SH_ONE * dir_x,
        SH_TWO[0] * dir_x * dir_y,
        SH_TWO[1] * dir_y * dir_z,
        SH_TWO[2] * (2.0 * sq_z - sq_x - sq_y),
        SH_TWO[3] * dir_x * dir_z,
        SH_TWO[4] * (sq_x - sq_y),
        SH_THREE[0] * dir_y * (3.0 * sq_x - sq_y),
        SH_THREE[1] * dir_x * dir_y * dir_z,
        SH_THREE[2] * dir_y * (4.0 * sq_z - sq_x - sq_y),
        SH_THREE[3] * dir_z * (2.0 * sq_z - 3.0 * sq_x - 3.0 * sq_y),
        SH_THREE[4] * dir_x * (4.0 * sq_z - sq_x - sq_y),
        SH_THREE[5] * dir_z * (sq_x - sq_y),
        SH_THREE[6] * dir_x * (sq_x - 3.0 * sq_y),
    ]


def project(rows, camera):
    focal_x, focal_y, centre_x, centre_y = camera
    mean_x, mean_y, mean_z = rows[0:3]
    spread = [jnp.exp(row) for row in rows[3:6]]
    q_w, q_x, q_y, q_z = rows[6:10]
    scale = lax.rsqrt(q_w * q_w + q_x * q_x + q_y * q_y + q_z * q_z)
    w_part, x_part, y_part, z_part = (q_w * scale, q_x * scale, q_y * scale, q_z * scale)
    rotate = [
        [
            1.0 - 2.0 * (y_part * y_part + z_part * z_part),
            2.0 * (x_part * y_part - w_part * z_part),
            2.0 * (x_part * z_part + w_part * y_part),
        ],
        [
            2.0 * (x_part * y_part + w_part * z_part),
            1.0 - 2.0 * (x_part * x_part + z_part * z_part),
            2.0 * (y_part * z_part - w_part * x_part),
        ],
        [
            2.0 * (x_part * z_part - w_part * y_part),
            2.0 * (y_part * z_part + w_part * x_part),
            1.0 - 2.0 * (x_part * x_part + y_part * y_part),
        ],
    ]
    depth_inv = 1.0 / mean_z
    along_x = mean_x * depth_inv
    along_y = mean_y * depth_inv
    lens_x = focal_x * depth_inv
    lens_y = focal_y * depth_inv
    first = [lens_x * (rotate[0][c] - along_x * rotate[2][c]) * spread[c] for c in range(3)]
    second = [lens_y * (rotate[1][c] - along_y * rotate[2][c]) * spread[c] for c in range(3)]
    cov_a = first[0] * first[0] + first[1] * first[1] + first[2] * first[2] + 0.3
    cov_b = first[0] * second[0] + first[1] * second[1] + first[2] * second[2]
    cov_c = second[0] * second[0] + second[1] * second[1] + second[2] * second[2] + 0.3
    inverse = LOG2E / (cov_a * cov_c - cov_b * cov_b)
    conic_a = -0.5 * cov_c * inverse
    conic_b = cov_b * inverse
    conic_c = -0.5 * cov_a * inverse
    screen_x = focal_x * along_x + centre_x
    screen_y = focal_y * along_y + centre_y
    opacity = -LOG2E * jnp.log(1.0 + jnp.exp(-rows[10]))
    radius = lax.rsqrt(mean_x * mean_x + mean_y * mean_y + mean_z * mean_z)
    basis = harmonics(mean_x * radius, mean_y * radius, mean_z * radius)
    colours = []
    for k in range(3):
        total = SH_ZERO * rows[11 + 16 * k] + 0.5
        for j in range(1, 16):
            total = total + basis[j] * rows[11 + 16 * k + j]
        colours.append(jnp.maximum(total, 0.0))
    return [screen_x, screen_y, conic_a, conic_b, conic_c, opacity] + colours


def low_half(shape):
    return lax.broadcasted_iota(jnp.int32, shape, len(shape) - 1) < 64


def swap(values):
    return pltpu.roll(values, 64, axis=1)


def spread_tiles(gaussians_ref, flat_ref):
    def body(t, carry):
        lanes = pl.ds(pl.multiple_of(t * 128, 128), 128)
        for g in range(8):
            size = 8 if g < 7 else 3
            start = pl.multiple_of((g * 64 + t) * 8, 8)
            flat_ref[pl.ds(start, size), :] = gaussians_ref[8 * g : 8 * g + size, lanes]
        return carry

    lax.fori_loop(0, 64, body, 0, unroll=4)


def param_rows(flat_ref, chunk, size):
    return [
        flat_ref[pl.ds((k // 8) * 512 + k % 8 + chunk * size * 8, size, stride=8), :]
        for k in range(59)
    ]


def parts(values, count):
    out = []
    for step in range(count):
        piece = values.astype(jnp.bfloat16)
        out.append(piece)
        if step + 1 < count:
            values = values - piece.astype(jnp.float32)
    return out


def pack_table(table_ref, packed_ref):
    extra = 2 * FEATS
    for f in range(FEATS):
        whole = jnp.concatenate(
            [table_ref[f, pl.ds(0, 32, stride=2), :], table_ref[f, pl.ds(1, 32, stride=2), :]], axis=1
        )
        pieces = parts(whole, 3 if f in TRIPLE else 2)
        packed_ref[64 * f : 64 * f + 32, :] = pieces[0]
        packed_ref[64 * f + 32 : 64 * f + 64, :] = pieces[1]
        if f in TRIPLE:
            packed_ref[32 * extra : 32 * extra + 32, :] = pieces[2]
            extra += 1


def one_hot(index):
    count = index.shape[1]
    rows = lax.broadcasted_iota(jnp.int32, (256, count), 0)
    return jnp.where(rows == (index & 255), 1.0, 0.0).astype(jnp.bfloat16)


def upper_mask(index):
    count = index.shape[1]
    rows = lax.broadcasted_iota(jnp.int32, (32, count), 0)
    return jnp.where(rows == (index >> 8), 1.0, 0.0)


def gather_features(packed_ref, index):
    mask = upper_mask(index)
    found = jnp.dot(packed_ref[...], one_hot(index), preferred_element_type=jnp.float32)
    out = []
    extra = 2 * FEATS
    for f in range(FEATS):
        block = found[64 * f : 64 * f + 32] + found[64 * f + 32 : 64 * f + 64]
        if f in TRIPLE:
            block = block + found[32 * extra : 32 * extra + 32]
            extra += 1
        out.append(jnp.sum(block * mask, axis=0, keepdims=True))
    return out


def one_hot_rows(column):
    lanes = lax.broadcasted_iota(jnp.int32, (column.shape[0], 256), 1)
    return jnp.where(lanes == (column.astype(jnp.int32) & 255), 1.0, 0.0).astype(jnp.bfloat16)


def scatter_features(total_ref, rows, index, column):
    mask = upper_mask(index).astype(jnp.bfloat16)
    blocks = []
    for row in rows:
        for piece in parts(row, 2):
            blocks.append(mask * piece)
    total_ref[...] += jnp.dot(
        jnp.concatenate(blocks, axis=0), one_hot_rows(column), preferred_element_type=jnp.float32
    )


def unpack_total(total_ref, table_ref):
    for f in range(FEATS):
        whole = total_ref[64 * f : 64 * f + 32, :] + total_ref[64 * f + 32 : 64 * f + 64, :]
        table_ref[f, pl.ds(0, 32, stride=2), :] = whole[:, :128]
        table_ref[f, pl.ds(1, 32, stride=2), :] = whole[:, 128:]


def table_to_blocks(table_ref, out_ref):
    low = low_half((64, 128))
    for i in range(5):
        even = table_ref[2 * i]
        odd = table_ref[2 * i + 1] if 2 * i + 1 < FEATS else jnp.zeros((64, 128), jnp.float32)
        out_ref[pl.ds(i, 64, stride=10), :] = jnp.where(low, even, swap(odd))
        out_ref[pl.ds(5 + i, 64, stride=10), :] = jnp.where(low, swap(even), odd)


def blocks_to_table(in_ref, table_ref):
    low = low_half((64, 128))
    for i in range(5):
        first = in_ref[pl.ds(i, 64, stride=10), :]
        second = in_ref[pl.ds(5 + i, 64, stride=10), :]
        table_ref[2 * i] = jnp.where(low, first, swap(second))
        if 2 * i + 1 < FEATS:
            table_ref[2 * i + 1] = jnp.where(low, swap(first), second)


def row_of(ref, q):
    return jnp.concatenate([ref[pl.ds(4 * q + c, 1), :] for c in range(4)], axis=1)


CHUNK = 8


def project_kernel(camera_ref, gaussians_ref, packed_ref, flat_ref, table_ref):
    camera = [camera_ref[k] for k in range(4)]
    spread_tiles(gaussians_ref, flat_ref)

    def body(chunk, carry):
        features = project(param_rows(flat_ref, chunk, CHUNK), camera)
        for f in range(FEATS):
            table_ref[f, pl.ds(pl.multiple_of(chunk * CHUNK, CHUNK), CHUNK), :] = features[f]
        return carry

    lax.fori_loop(0, 64 // CHUNK, body, 0)
    pack_table(table_ref, packed_ref)


def fetch_kernel(parity_ref, packed_ref, asked_ref, index_ref, send_ref, table_ref):
    low = low_half((64, 128))
    even = asked_ref[pl.ds(0, 64, stride=2), :]
    odd = asked_ref[pl.ds(1, 64, stride=2), :]
    index_ref[...] = jnp.where(
        parity_ref[0] == 0,
        jnp.where(low, even, swap(odd)),
        jnp.where(low, swap(even), odd),
    )

    def body(q, carry):
        rows = gather_features(packed_ref, row_of(index_ref, q))
        for f in range(FEATS):
            for c in range(4):
                table_ref[f, pl.ds(4 * q + c, 1), :] = rows[f][:, 128 * c : 128 * c + 128]
        return carry

    lax.fori_loop(0, 16, body, 0)
    table_to_blocks(table_ref, send_ref)


def return_kernel(camera_ref, gaussians_ref, index_ref, back_ref, grads_ref, flat_ref, table_ref, total_ref):
    camera = [camera_ref[k] for k in range(4)]
    spread_tiles(gaussians_ref, flat_ref)
    blocks_to_table(back_ref, table_ref)
    total_ref[...] = jnp.zeros_like(total_ref)
    columns = jnp.concatenate([index_ref[...].astype(jnp.float32), jnp.zeros((64, 128), jnp.float32)], axis=0).T
    for q in range(16):
        rows = [row_of(table_ref.at[f], q) for f in range(FEATS)]
        column = jnp.concatenate([columns[:, 4 * q + c : 4 * q + c + 1] for c in range(4)], axis=0)
        scatter_features(total_ref, rows, row_of(index_ref, q), column)
    unpack_total(total_ref, table_ref)

    def body(chunk, carry):
        params = param_rows(flat_ref, chunk, CHUNK)
        _, pullback = jax.vjp(lambda rows: project(rows, camera), params)
        place = pl.ds(pl.multiple_of(chunk * CHUNK, CHUNK), CHUNK)
        (grads,) = pullback([table_ref[f, place, :] for f in range(FEATS)])
        for k in range(59):
            start = (k // 8) * 512 + k % 8 + chunk * CHUNK * 8
            flat_ref[pl.ds(start, CHUNK, stride=8), :] = grads[k]
        return carry

    lax.fori_loop(0, 64 // CHUNK, body, 0)

    def out(t, carry):
        lanes = pl.ds(pl.multiple_of(t * 128, 128), 128)
        for g in range(8):
            size = 8 if g < 7 else 3
            start = pl.multiple_of((g * 64 + t) * 8, 8)
            grads_ref[8 * g : 8 * g + size, lanes] = flat_ref[pl.ds(start, size), :]
        return carry

    lax.fori_loop(0, 64, out, 0, unroll=4)


def monomials():
    lane = lax.broadcasted_iota(jnp.int32, (1, 256), 1)
    x = (lane & 15).astype(jnp.float32) - 7.5
    y = (lane >> 4).astype(jnp.float32) - 7.5
    return [jnp.ones((1, 256), jnp.float32), x, y, x * x, x * y, y * y]


def render_kernel(
    ids_ref,
    counts_ref,
    active_ref,
    recv_ref,
    lists_ref,
    target_ref,
    image_ref,
    send_ref,
    seg_tile,
    seg_place,
    table_ref,
    packed_ref,
    total_ref,
    basis_ref,
    moment_ref,
    index_ref,
    shape_ref,
    coef_ref,
    wide_ref,
    power_ref,
    alpha_ref,
    weight_ref,
    pass_ref,
    light_ref,
    start_ref,
    behind_ref,
    resid_ref,
    resid_rows_ref,
    pieces_ref,
    sums_ref,
):
    def clear(n, carry):
        seg_tile[n] = 0
        seg_place[n] = 16
        return carry

    lax.fori_loop(0, SEGS * MAX_GROUPS, clear, 0)

    def add_tile(t, n):
        used = jnp.where(active_ref[0, t] > 0, (counts_ref[0, t] + (SEG - 1)) >> 6, 0)

        def add_segment(k, m):
            seg_tile[m] = t
            seg_place[m] = k
            return m + 1

        return lax.fori_loop(0, used, add_segment, n)

    segments = lax.fori_loop(0, 16, add_tile, 0)
    groups = (segments + (SEGS - 1)) // SEGS

    blocks_to_table(recv_ref, table_ref)
    pack_table(table_ref, packed_ref)
    total_ref[...] = jnp.zeros_like(total_ref)
    pass_ref[...] = jnp.ones_like(pass_ref)
    light_ref[...] = jnp.zeros_like(light_ref)
    coef_ref[...] = jnp.zeros_like(coef_ref)
    start_ref[256:272, :] = jnp.zeros((16, 256), jnp.float32)
    behind_ref[256:272, :] = jnp.zeros((16, 256), jnp.float32)
    terms = monomials()
    basis_rows = terms * 3 + [jnp.zeros((1, 256), jnp.float32)] * 14
    basis_ref[...] = jnp.concatenate(basis_rows, axis=0).astype(jnp.bfloat16)
    resid_rows_ref[...] = jnp.zeros_like(resid_rows_ref)
    flat = jnp.concatenate(terms + [jnp.zeros((1, 256), jnp.float32)] * 122, axis=0)
    for half in range(2):
        turned = flat[:, 128 * half : 128 * half + 128].T.astype(jnp.bfloat16)
        moment_ref[128 * half : 128 * half + 128, :] = turned
        moment_ref[256 + 128 * half : 384 + 128 * half, :] = turned

    low = low_half((1, 128))
    lane = lax.broadcasted_iota(jnp.int32, (1, 128), 1) & 63

    def forward(g, carry):
        index, keep, mid_x, mid_y = [], [], [], []
        for c in range(SEGS // 2):
            pair = []
            for half in range(2):
                n = SEGS * g + 2 * c + half
                t, place = seg_tile[n], seg_place[n]
                near = jnp.minimum(place, 15)
                row = lists_ref[pl.ds(t * 8 + (near >> 1), 1), :]
                row = jnp.where((near & 1) == half, row, swap(row))
                screen = ids_ref[0, t]
                pair.append(
                    (
                        row,
                        counts_ref[0, t] - place * SEG,
                        ((screen & 63) * 16 + 8).astype(jnp.float32),
                        ((screen >> 6) * 16 + 8).astype(jnp.float32),
                    )
                )
            index.append(jnp.where(low, pair[0][0], pair[1][0]))
            keep.append(lane < jnp.where(low, pair[0][1], pair[1][1]))
            mid_x.append(jnp.where(low, pair[0][2], pair[1][2]))
            mid_y.append(jnp.where(low, pair[0][3], pair[1][3]))
        index = jnp.concatenate(index, axis=1)
        keep = jnp.concatenate([jnp.where(part, 1.0, 0.0) for part in keep], axis=1) > 0.5
        mid_x = jnp.concatenate(mid_x, axis=1)
        mid_y = jnp.concatenate(mid_y, axis=1)
        index_ref[pl.ds(g, 1), :] = index
        found = gather_features(packed_ref, index)
        at_x = found[0] - mid_x
        at_y = found[1] - mid_y
        con_a, con_b, con_c, opacity = found[2:6]
        shape_ref[g, :, :] = jnp.concatenate([at_x, at_y, con_a, con_b, con_c, opacity, opacity, opacity], axis=0)
        line_x = -2.0 * con_a * at_x - con_b * at_y
        line_y = -2.0 * con_c * at_y - con_b * at_x
        level = opacity - 0.5 * (line_x * at_x + line_y * at_y)
        coefs = [jnp.where(keep, level, -30000.0)]
        coefs += [jnp.where(keep, row, 0.0) for row in (line_x, line_y, con_a, con_b, con_c)]
        for j in range(6):
            pieces = parts(coefs[j], 3)
            for step in range(3):
                coef_ref[6 * step + j : 6 * step + j + 1, :] = pieces[step].astype(jnp.float32)
        for k in range(3):
            coef_ref[18 + k : 19 + k, :] = found[6 + k]
        coef_ref[21:22, :] = index.astype(jnp.float32)
        first = pl.multiple_of(g * GROUP, GROUP)
        for c in range(GROUP // 128):
            wide_ref[pl.ds(first + 128 * c, 128), :] = coef_ref[:, 128 * c : 128 * c + 128].T
        rows = wide_ref[pl.ds(first, GROUP), :].astype(jnp.bfloat16)
        power = jnp.dot(rows, basis_ref[...], preferred_element_type=jnp.float32)
        power_ref[0, :, :] = power[:, :128]
        power_ref[1, :, :] = power[:, 128:]

        def block(b, state):
            transmit, red, green, blue = state
            for u in range(STEPS):
                i = b * STEPS + u
                here = pl.multiple_of(b * (STEPS * SEGS), STEPS * SEGS) + SEGS * u
                power = [power_ref[half, pl.ds(i, SEGS, stride=SEG), :] for half in range(2)]
                alpha = jnp.exp2(jnp.concatenate(power, axis=1))
                weight = alpha * transmit
                transmit = transmit - weight
                alpha_ref[pl.ds(first + here, SEGS), :] = alpha
                weight_ref[pl.ds(first + here, SEGS), :] = weight
                tint = wide_ref[pl.ds(first + i, SEGS, stride=SEG), :]
                red = red + weight * tint[:, 18:19]
                green = green + weight * tint[:, 19:20]
                blue = blue + weight * tint[:, 20:21]
            return (transmit, red, green, blue)

        zero = jnp.zeros((SEGS, 256), jnp.float32)
        transmit, *lights = lax.fori_loop(
            0, SEG // STEPS, block, (jnp.ones((SEGS, 256), jnp.float32), zero, zero, zero)
        )
        for s in range(SEGS):
            n = SEGS * g + s
            spot = seg_place[n] * 16 + seg_tile[n]
            pass_ref[pl.ds(spot, 1), :] = transmit[s : s + 1]
            for k in range(3):
                light_ref[k, pl.ds(spot, 1), :] = lights[k][s : s + 1]
        return carry

    lax.fori_loop(0, groups, forward, 0)

    transmit = jnp.ones((16, 256), jnp.float32)
    image = [jnp.zeros((16, 256), jnp.float32) for _ in range(3)]
    for place in range(16):
        span = slice(16 * place, 16 * place + 16)
        start_ref[span, :] = transmit
        image = [image[k] + transmit * light_ref[k, span, :] for k in range(3)]
        transmit = transmit * pass_ref[span, :]
    resid = []
    for k in range(3):
        image_ref[k] = image[k]
        resid.append(image[k] - target_ref[k])
        resid_ref[k] = resid[k]
    behind = jnp.zeros((16, 256), jnp.float32)
    for place in reversed(range(16)):
        span = slice(16 * place, 16 * place + 16)
        behind_ref[span, :] = behind
        own = sum(resid[k] * light_ref[k, span, :] for k in range(3))
        behind = own + pass_ref[span, :] * behind

    segment = lax.broadcasted_iota(jnp.int32, (SEGS, GROUP), 0)
    own_lane = segment == (lax.broadcasted_iota(jnp.int32, (SEGS, GROUP), 1) >> 6)

    def backward(g, carry):
        first = pl.multiple_of(g * GROUP, GROUP)
        tiles = [seg_tile[SEGS * g + s] for s in range(SEGS)]
        spots = [seg_place[SEGS * g + s] * 16 + tiles[s] for s in range(SEGS)]

        def rows_at(ref, places):
            return jnp.concatenate([ref[pl.ds(place, 1), :] for place in places], axis=0)

        start = rows_at(start_ref, spots)
        behind = rows_at(behind_ref, spots)
        resid = [rows_at(resid_ref.at[k], tiles) for k in range(3)]
        for k in range(3):
            high, rest = parts(resid[k], 2)
            resid_rows_ref[16 + 16 * k : 32 + 16 * k, :] = high.astype(jnp.float32)
            resid_rows_ref[64 + 16 * k : 80 + 16 * k, :] = rest.astype(jnp.float32)
        for half in range(2):
            turned = resid_rows_ref[:, 128 * half : 128 * half + 128].T.astype(jnp.bfloat16)
            moment_ref[512 + 128 * half : 640 + 128 * half, :] = turned
            moment_ref[768 + 128 * half : 896 + 128 * half, :] = turned

        def block(step, behind):
            b = SEG // STEPS - 1 - step
            at = pl.multiple_of(b * (STEPS * SEGS), STEPS * SEGS)
            for u in reversed(range(STEPS)):
                i = b * STEPS + u
                here = first + at + SEGS * u
                tint = wide_ref[pl.ds(first + i, SEGS, stride=SEG), :]
                shade = resid[0] * tint[:, 18:19] + resid[1] * tint[:, 19:20] + resid[2] * tint[:, 20:21]
                ahead = shade - behind
                behind = behind + alpha_ref[pl.ds(here, SEGS), :] * ahead
                weight = start * weight_ref[pl.ds(here, SEGS), :]
                for k, values in enumerate((weight * ahead, weight)):
                    high, rest = parts(values, 2)
                    pieces_ref[pl.ds(at + SEGS * u, SEGS), 512 * k : 512 * k + 256] = high
                    pieces_ref[pl.ds(at + SEGS * u, SEGS), 512 * k + 256 : 512 * k + 512] = rest
            return behind

        lax.fori_loop(0, SEG // STEPS, block, behind)
        sums_ref[...] = jnp.dot(pieces_ref[...], moment_ref[...], preferred_element_type=jnp.float32)
        turned = []
        for c in range(SEGS // 2):
            both = [sums_ref[pl.ds(2 * c + half, SEG, stride=SEGS), :] for half in range(2)]
            turned.append(jnp.concatenate(both, axis=0).T)
        turned = jnp.concatenate(turned, axis=1)
        m_0, m_x, m_y, m_xx, m_xy, m_yy = [LN2 * turned[j : j + 1] for j in range(6)]
        at_x, at_y, con_a, con_b, con_c = [shape_ref[g, j : j + 1, :] for j in range(5)]
        s_x = m_x - at_x * m_0
        s_y = m_y - at_y * m_0
        s_xx = m_xx - at_x * (m_x + s_x)
        s_xy = m_xy - at_x * m_y - at_y * s_x
        s_yy = m_yy - at_y * (m_y + s_y)
        rows = [
            -(2.0 * con_a * s_x + con_b * s_y),
            -(2.0 * con_c * s_y + con_b * s_x),
            s_xx,
            s_xy,
            s_yy,
            m_0,
        ]
        for k in range(3):
            both = turned[16 + 16 * k : 32 + 16 * k] + turned[64 + 16 * k : 80 + 16 * k]
            rows.append(jnp.sum(jnp.where(own_lane, both, 0.0), axis=0, keepdims=True))
        column = wide_ref[pl.ds(first, GROUP), :][:, 21:22]
        scatter_features(total_ref, rows, index_ref[pl.ds(g, 1), :], column)
        return carry

    lax.fori_loop(0, groups, backward, 0)
    unpack_total(total_ref, table_ref)
    table_to_blocks(table_ref, send_ref)


def smem():
    return pl.BlockSpec(memory_space=pltpu.SMEM)


def vmem():
    return pl.BlockSpec(memory_space=pltpu.VMEM)


def limits(mib):
    return pltpu.CompilerParams(vmem_limit_bytes=mib * 1024 * 1024)


def run_project(camera, gaussians):
    return pl.pallas_call(
        project_kernel,
        out_shape=jax.ShapeDtypeStruct((ROWS, 256), jnp.bfloat16),
        in_specs=[smem(), vmem()],
        out_specs=vmem(),
        scratch_shapes=[pltpu.VMEM((4096, 128), jnp.float32), pltpu.VMEM((FEATS, 64, 128), jnp.float32)],
        compiler_params=limits(16),
        name="project",
    )(camera, gaussians)


def run_fetch(parity, packed, asked):
    return pl.pallas_call(
        fetch_kernel,
        out_shape=(
            jax.ShapeDtypeStruct((64, 128), jnp.int32),
            jax.ShapeDtypeStruct((640, 128), jnp.float32),
        ),
        in_specs=[smem(), vmem(), vmem()],
        out_specs=(vmem(), vmem()),
        scratch_shapes=[pltpu.VMEM((FEATS, 64, 128), jnp.float32)],
        compiler_params=limits(16),
        name="fetch",
    )(parity, packed, asked)


def run_render(tile_ids, counts, active, received, lists, target):
    f32, bf16 = jnp.float32, jnp.bfloat16
    entries = MAX_GROUPS * GROUP
    return pl.pallas_call(
        render_kernel,
        out_shape=(
            jax.ShapeDtypeStruct((3, 16, 256), f32),
            jax.ShapeDtypeStruct((640, 128), f32),
        ),
        in_specs=[smem(), smem(), smem(), vmem(), vmem(), vmem()],
        out_specs=(vmem(), vmem()),
        scratch_shapes=[
            pltpu.SMEM((SEGS * MAX_GROUPS,), jnp.int32),
            pltpu.SMEM((SEGS * MAX_GROUPS,), jnp.int32),
            pltpu.VMEM((FEATS, 64, 128), f32),
            pltpu.VMEM((ROWS, 256), bf16),
            pltpu.VMEM((BACK_ROWS, 256), f32),
            pltpu.VMEM((32, 256), bf16),
            pltpu.VMEM((1024, 128), bf16),
            pltpu.VMEM((16, GROUP), jnp.int32),
            pltpu.VMEM((MAX_GROUPS, 8, GROUP), f32),
            pltpu.VMEM((32, GROUP), f32),
            pltpu.VMEM((entries, 32), f32),
            pltpu.VMEM((2, GROUP, 128), f32),
            pltpu.VMEM((entries, 256), f32),
            pltpu.VMEM((entries, 256), f32),
            pltpu.VMEM((272, 256), f32),
            pltpu.VMEM((3, 272, 256), f32),
            pltpu.VMEM((272, 256), f32),
            pltpu.VMEM((272, 256), f32),
            pltpu.VMEM((3, 16, 256), f32),
            pltpu.VMEM((128, 256), f32),
            pltpu.VMEM((GROUP, 1024), bf16),
            pltpu.VMEM((GROUP, 128), f32),
        ],
        compiler_params=limits(48),
        name="render",
    )(tile_ids, counts, active, received, lists, target)


def run_return(camera, gaussians, index, back):
    return pl.pallas_call(
        return_kernel,
        out_shape=jax.ShapeDtypeStruct((59, 8192), jnp.float32),
        in_specs=[smem(), vmem(), vmem(), vmem()],
        out_specs=vmem(),
        scratch_shapes=[
            pltpu.VMEM((4096, 128), jnp.float32),
            pltpu.VMEM((FEATS, 64, 128), jnp.float32),
            pltpu.VMEM((BACK_ROWS, 256), jnp.float32),
        ],
        compiler_params=limits(24),
        name="give_back",
    )(camera, gaussians, index, back)


def exchange(rows):
    count = rows.shape[0] // 128 * rows.shape[1]
    moved = lax.all_to_all(rows.reshape(128, 1, count), AXES, split_axis=0, concat_axis=0, tiled=True)
    return moved.reshape(rows.shape)


def local(gaussians, camera, asked, parity, tile_ids, tile_lists, tile_counts, tile_active, target, send_on):
    lists = tile_lists.reshape(128, 128)
    packed = run_project(camera, gaussians)
    index, send = run_fetch(parity, packed, asked)
    image, back = run_render(tile_ids, tile_counts, tile_active, send_on(send), lists, target)
    grads = run_return(camera, gaussians, index, send_on(back))
    return (image, grads)


def per_device(gaussians, camera, fetch_index, tile_ids, tile_lists, tile_counts, tile_active, target):
    asked = exchange(jnp.repeat(fetch_index.reshape(64, 128), 2, axis=0))
    parity = (lax.axis_index("shard") % 2).astype(jnp.int32).reshape(1)
    return local(gaussians, camera, asked, parity, tile_ids, tile_lists, tile_counts, tile_active, target, exchange)


def solution(mesh):
    in_specs = (
        P(None, AXES),
        P(),
        P(AXES, None),
        P(AXES, None),
        P(AXES, None, None),
        P(AXES, None),
        P(AXES, None),
        P(None, AXES, None),
    )
    out_specs = (P(None, AXES, None), P(None, AXES))
    return jax.shard_map(per_device, mesh=mesh, in_specs=in_specs, out_specs=out_specs, check_vma=False)
```

```python
import functools

import jax
import jax.numpy as jnp
from jax import lax
from jax.experimental import pallas as pl
from jax.experimental.pallas import tpu as pltpu
from jax.sharding import PartitionSpec as P

AXES = ("tile", "shard")
SEG = 64
SEGS = 16
GROUP = SEG * SEGS
MAX_GROUPS = 9
LOG2E = 1.4426950408889634
LN2 = 0.6931471805599453
FEATS = 9
TRIPLE = (0, 1)
ROWS = 32 * (2 * FEATS + len(TRIPLE))
BACK_ROWS = 32 * 2 * FEATS

SH_ZERO = 0.28209479177387814
SH_ONE = 0.4886025119029199
SH_TWO = (
    1.0925484305920792,
    -1.0925484305920792,
    0.31539156525252005,
    -1.0925484305920792,
    0.5462742152960396,
)
SH_THREE = (
    -0.5900435899266435,
    2.890611442640554,
    -0.4570457994644658,
    0.3731763325901154,
    -0.4570457994644658,
    1.445305721320277,
    -0.5900435899266435,
)


def harmonics(dir_x, dir_y, dir_z):
    sq_x, sq_y, sq_z = (dir_x * dir_x, dir_y * dir_y, dir_z * dir_z)
    return [
        None,
        -SH_ONE * dir_y,
        SH_ONE * dir_z,
        -SH_ONE * dir_x,
        SH_TWO[0] * dir_x * dir_y,
        SH_TWO[1] * dir_y * dir_z,
        SH_TWO[2] * (2.0 * sq_z - sq_x - sq_y),
        SH_TWO[3] * dir_x * dir_z,
        SH_TWO[4] * (sq_x - sq_y),
        SH_THREE[0] * dir_y * (3.0 * sq_x - sq_y),
        SH_THREE[1] * dir_x * dir_y * dir_z,
        SH_THREE[2] * dir_y * (4.0 * sq_z - sq_x - sq_y),
        SH_THREE[3] * dir_z * (2.0 * sq_z - 3.0 * sq_x - 3.0 * sq_y),
        SH_THREE[4] * dir_x * (4.0 * sq_z - sq_x - sq_y),
        SH_THREE[5] * dir_z * (sq_x - sq_y),
        SH_THREE[6] * dir_x * (sq_x - 3.0 * sq_y),
    ]


def project(rows, camera):
    focal_x, focal_y, centre_x, centre_y = camera
    mean_x, mean_y, mean_z = rows[0:3]
    spread = [jnp.exp(row) for row in rows[3:6]]
    q_w, q_x, q_y, q_z = rows[6:10]
    scale = lax.rsqrt(q_w * q_w + q_x * q_x + q_y * q_y + q_z * q_z)
    w_part, x_part, y_part, z_part = (q_w * scale, q_x * scale, q_y * scale, q_z * scale)
    rotate = [
        [
            1.0 - 2.0 * (y_part * y_part + z_part * z_part),
            2.0 * (x_part * y_part - w_part * z_part),
            2.0 * (x_part * z_part + w_part * y_part),
        ],
        [
            2.0 * (x_part * y_part + w_part * z_part),
            1.0 - 2.0 * (x_part * x_part + z_part * z_part),
            2.0 * (y_part * z_part - w_part * x_part),
        ],
        [
            2.0 * (x_part * z_part - w_part * y_part),
            2.0 * (y_part * z_part + w_part * x_part),
            1.0 - 2.0 * (x_part * x_part + y_part * y_part),
        ],
    ]
    depth_inv = 1.0 / mean_z
    along_x = mean_x * depth_inv
    along_y = mean_y * depth_inv
    lens_x = focal_x * depth_inv
    lens_y = focal_y * depth_inv
    first = [lens_x * (rotate[0][c] - along_x * rotate[2][c]) * spread[c] for c in range(3)]
    second = [lens_y * (rotate[1][c] - along_y * rotate[2][c]) * spread[c] for c in range(3)]
    cov_a = first[0] * first[0] + first[1] * first[1] + first[2] * first[2] + 0.3
    cov_b = first[0] * second[0] + first[1] * second[1] + first[2] * second[2]
    cov_c = second[0] * second[0] + second[1] * second[1] + second[2] * second[2] + 0.3
    inverse = LOG2E / (cov_a * cov_c - cov_b * cov_b)
    conic_a = -0.5 * cov_c * inverse
    conic_b = cov_b * inverse
    conic_c = -0.5 * cov_a * inverse
    screen_x = focal_x * along_x + centre_x
    screen_y = focal_y * along_y + centre_y
    opacity = -LOG2E * jnp.log(1.0 + jnp.exp(-rows[10]))
    radius = lax.rsqrt(mean_x * mean_x + mean_y * mean_y + mean_z * mean_z)
    basis = harmonics(mean_x * radius, mean_y * radius, mean_z * radius)
    colours = []
    for k in range(3):
        total = SH_ZERO * rows[11 + 16 * k] + 0.5
        for j in range(1, 16):
            total = total + basis[j] * rows[11 + 16 * k + j]
        colours.append(jnp.maximum(total, 0.0))
    return [screen_x, screen_y, conic_a, conic_b, conic_c, opacity] + colours


def low_half(shape):
    return lax.broadcasted_iota(jnp.int32, shape, len(shape) - 1) < 64


def swap(values):
    return pltpu.roll(values, 64, axis=1)


def spread_tiles(gaussians_ref, flat_ref):
    def body(t, carry):
        lanes = pl.ds(pl.multiple_of(t * 128, 128), 128)
        for g in range(8):
            size = 8 if g < 7 else 3
            start = pl.multiple_of((g * 64 + t) * 8, 8)
            flat_ref[pl.ds(start, size), :] = gaussians_ref[8 * g : 8 * g + size, lanes]
        return carry

    lax.fori_loop(0, 64, body, 0, unroll=4)


def param_rows(flat_ref, chunk, size):
    return [
        flat_ref[pl.ds((k // 8) * 512 + k % 8 + chunk * size * 8, size, stride=8), :]
        for k in range(59)
    ]


def parts(values, count):
    out = []
    for step in range(count):
        piece = values.astype(jnp.bfloat16)
        out.append(piece)
        if step + 1 < count:
            values = values - piece.astype(jnp.float32)
    return out


def pack_table(table_ref, packed_ref):
    extra = 2 * FEATS
    for f in range(FEATS):
        whole = jnp.concatenate(
            [table_ref[f, pl.ds(0, 32, stride=2), :], table_ref[f, pl.ds(1, 32, stride=2), :]], axis=1
        )
        pieces = parts(whole, 3 if f in TRIPLE else 2)
        packed_ref[64 * f : 64 * f + 32, :] = pieces[0]
        packed_ref[64 * f + 32 : 64 * f + 64, :] = pieces[1]
        if f in TRIPLE:
            packed_ref[32 * extra : 32 * extra + 32, :] = pieces[2]
            extra += 1


def one_hot(index):
    count = index.shape[1]
    rows = lax.broadcasted_iota(jnp.int32, (256, count), 0)
    return jnp.where(rows == (index & 255), 1.0, 0.0).astype(jnp.bfloat16)


def upper_mask(index):
    count = index.shape[1]
    rows = lax.broadcasted_iota(jnp.int32, (32, count), 0)
    return jnp.where(rows == (index >> 8), 1.0, 0.0)


def gather_features(packed_ref, index):
    mask = upper_mask(index)
    found = jnp.dot(packed_ref[...], one_hot(index), preferred_element_type=jnp.float32)
    out = []
    extra = 2 * FEATS
    for f in range(FEATS):
        block = found[64 * f : 64 * f + 32] + found[64 * f + 32 : 64 * f + 64]
        if f in TRIPLE:
            block = block + found[32 * extra : 32 * extra + 32]
            extra += 1
        out.append(jnp.sum(block * mask, axis=0, keepdims=True))
    return out


def one_hot_rows(column):
    lanes = lax.broadcasted_iota(jnp.int32, (column.shape[0], 256), 1)
    return jnp.where(lanes == (column.astype(jnp.int32) & 255), 1.0, 0.0).astype(jnp.bfloat16)


def scatter_features(total_ref, rows, index, column):
    mask = upper_mask(index).astype(jnp.bfloat16)
    blocks = []
    for row in rows:
        for piece in parts(row, 2):
            blocks.append(mask * piece)
    total_ref[...] += jnp.dot(
        jnp.concatenate(blocks, axis=0), one_hot_rows(column), preferred_element_type=jnp.float32
    )


def unpack_total(total_ref, table_ref):
    for f in range(FEATS):
        whole = total_ref[64 * f : 64 * f + 32, :] + total_ref[64 * f + 32 : 64 * f + 64, :]
        table_ref[f, pl.ds(0, 32, stride=2), :] = whole[:, :128]
        table_ref[f, pl.ds(1, 32, stride=2), :] = whole[:, 128:]


def table_to_blocks(table_ref, out_ref):
    low = low_half((64, 128))
    for i in range(5):
        even = table_ref[2 * i]
        odd = table_ref[2 * i + 1] if 2 * i + 1 < FEATS else jnp.zeros((64, 128), jnp.float32)
        out_ref[pl.ds(i, 64, stride=10), :] = jnp.where(low, even, swap(odd))
        out_ref[pl.ds(5 + i, 64, stride=10), :] = jnp.where(low, swap(even), odd)


def blocks_to_table(in_ref, table_ref):
    low = low_half((64, 128))
    for i in range(5):
        first = in_ref[pl.ds(i, 64, stride=10), :]
        second = in_ref[pl.ds(5 + i, 64, stride=10), :]
        table_ref[2 * i] = jnp.where(low, first, swap(second))
        if 2 * i + 1 < FEATS:
            table_ref[2 * i + 1] = jnp.where(low, swap(first), second)


def row_of(ref, q):
    return jnp.concatenate([ref[pl.ds(4 * q + c, 1), :] for c in range(4)], axis=1)


CHUNK = 8


def project_kernel(camera_ref, gaussians_ref, packed_ref, flat_ref, table_ref):
    camera = [camera_ref[k] for k in range(4)]
    spread_tiles(gaussians_ref, flat_ref)

    def body(chunk, carry):
        features = project(param_rows(flat_ref, chunk, CHUNK), camera)
        for f in range(FEATS):
            table_ref[f, pl.ds(pl.multiple_of(chunk * CHUNK, CHUNK), CHUNK), :] = features[f]
        return carry

    lax.fori_loop(0, 64 // CHUNK, body, 0)
    pack_table(table_ref, packed_ref)


def fetch_kernel(parity_ref, packed_ref, asked_ref, index_ref, send_ref, table_ref):
    low = low_half((64, 128))
    even = asked_ref[pl.ds(0, 64, stride=2), :]
    odd = asked_ref[pl.ds(1, 64, stride=2), :]
    index_ref[...] = jnp.where(
        parity_ref[0] == 0,
        jnp.where(low, even, swap(odd)),
        jnp.where(low, swap(even), odd),
    )

    for q in range(16):
        rows = gather_features(packed_ref, row_of(index_ref, q))
        for f in range(FEATS):
            for c in range(4):
                table_ref[f, 4 * q + c : 4 * q + c + 1, :] = rows[f][:, 128 * c : 128 * c + 128]
    table_to_blocks(table_ref, send_ref)


def return_kernel(camera_ref, gaussians_ref, index_ref, back_ref, grads_ref, flat_ref, table_ref, total_ref):
    camera = [camera_ref[k] for k in range(4)]
    spread_tiles(gaussians_ref, flat_ref)
    blocks_to_table(back_ref, table_ref)
    total_ref[...] = jnp.zeros_like(total_ref)
    columns = jnp.concatenate([index_ref[...].astype(jnp.float32), jnp.zeros((64, 128), jnp.float32)], axis=0).T
    for q in range(16):
        rows = [row_of(table_ref.at[f], q) for f in range(FEATS)]
        column = jnp.concatenate([columns[:, 4 * q + c : 4 * q + c + 1] for c in range(4)], axis=0)
        scatter_features(total_ref, rows, row_of(index_ref, q), column)
    unpack_total(total_ref, table_ref)

    def body(chunk, carry):
        params = param_rows(flat_ref, chunk, CHUNK)
        _, pullback = jax.vjp(lambda rows: project(rows, camera), params)
        place = pl.ds(pl.multiple_of(chunk * CHUNK, CHUNK), CHUNK)
        (grads,) = pullback([table_ref[f, place, :] for f in range(FEATS)])
        for k in range(59):
            start = (k // 8) * 512 + k % 8 + chunk * CHUNK * 8
            flat_ref[pl.ds(start, CHUNK, stride=8), :] = grads[k]
        return carry

    lax.fori_loop(0, 64 // CHUNK, body, 0)

    def out(t, carry):
        lanes = pl.ds(pl.multiple_of(t * 128, 128), 128)
        for g in range(8):
            size = 8 if g < 7 else 3
            start = pl.multiple_of((g * 64 + t) * 8, 8)
            grads_ref[8 * g : 8 * g + size, lanes] = flat_ref[pl.ds(start, size), :]
        return carry

    lax.fori_loop(0, 64, out, 0, unroll=4)


def monomials():
    lane = lax.broadcasted_iota(jnp.int32, (1, 256), 1)
    x = (lane & 15).astype(jnp.float32) - 7.5
    y = (lane >> 4).astype(jnp.float32) - 7.5
    return [jnp.ones((1, 256), jnp.float32), x, y, x * x, x * y, y * y]


def plan_kernel(counts_ref, active_ref, after_ref, seg_tile, seg_place, groups_ref):
    def clear(n, carry):
        seg_tile[n] = 0
        seg_place[n] = 16
        return carry

    lax.fori_loop(0, SEGS * (MAX_GROUPS + 1), clear, 0)

    def add_tile(t, n):
        used = jnp.where(active_ref[0, t] > 0, (counts_ref[0, t] + (SEG - 1)) >> 6, 0)

        def add_segment(k, m):
            seg_tile[m] = t
            seg_place[m] = k
            return m + 1

        return lax.fori_loop(0, used, add_segment, n)

    segments = lax.fori_loop(0, 16, add_tile, 0)
    groups_ref[0] = (segments + (SEGS - 1)) // SEGS


def render_kernel(
    ids_ref,
    counts_ref,
    seg_tile,
    seg_place,
    groups_ref,
    recv_ref,
    lists_ref,
    target_ref,
    image_ref,
    send_ref,
    table_ref,
    packed_ref,
    total_ref,
    basis_ref,
    moment_ref,
    coef_ref,
    plain_ref,
    wide_ref,
    power_a_ref,
    power_b_ref,
    tint_a_ref,
    tint_b_ref,
    alpha_ref,
    weight_ref,
    pass_ref,
    light_ref,
    start_ref,
    behind_ref,
    resid_ref,
    pieces_a_ref,
    pieces_b_ref,
):
    groups = groups_ref[0]
    blocks_to_table(recv_ref, table_ref)
    pack_table(table_ref, packed_ref)
    total_ref[...] = jnp.zeros_like(total_ref)
    pass_ref[...] = jnp.ones_like(pass_ref)
    light_ref[...] = jnp.zeros_like(light_ref)
    coef_ref[...] = jnp.zeros_like(coef_ref)
    start_ref[256:272, :] = jnp.zeros((16, 256), jnp.float32)
    behind_ref[256:272, :] = jnp.zeros((16, 256), jnp.float32)
    terms = monomials()
    basis_rows = terms * 3 + [jnp.zeros((1, 256), jnp.float32)] * 14
    basis_ref[...] = jnp.concatenate(basis_rows, axis=0).astype(jnp.bfloat16)
    flat = jnp.concatenate(terms + [jnp.zeros((1, 256), jnp.float32)] * 10, axis=0)
    moment_ref[...] = jnp.concatenate([flat, flat], axis=1).astype(jnp.bfloat16)

    low = low_half((1, 128))
    lane = lax.broadcasted_iota(jnp.int32, (1, 128), 1) & 63

    def prepare(g, power_ref, tint_ref):
        index, keep, mid_x, mid_y = [], [], [], []
        for c in range(SEGS // 2):
            pair = []
            for half in range(2):
                n = SEGS * g + 2 * c + half
                t, place = seg_tile[n], seg_place[n]
                near = jnp.minimum(place, 15)
                row = lists_ref[pl.ds(t * 8 + (near >> 1), 1), :]
                row = jnp.where((near & 1) == half, row, swap(row))
                screen = ids_ref[0, t]
                pair.append(
                    (
                        row,
                        counts_ref[0, t] - place * SEG,
                        ((screen & 63) * 16 + 8).astype(jnp.float32),
                        ((screen >> 6) * 16 + 8).astype(jnp.float32),
                    )
                )
            index.append(jnp.where(low, pair[0][0], pair[1][0]))
            keep.append(lane < jnp.where(low, pair[0][1], pair[1][1]))
            mid_x.append(jnp.where(low, pair[0][2], pair[1][2]))
            mid_y.append(jnp.where(low, pair[0][3], pair[1][3]))
        index = jnp.concatenate(index, axis=1)
        keep = jnp.concatenate([jnp.where(part, 1.0, 0.0) for part in keep], axis=1) > 0.5
        mid_x = jnp.concatenate(mid_x, axis=1)
        mid_y = jnp.concatenate(mid_y, axis=1)
        found = gather_features(packed_ref, index)
        at_x = found[0] - mid_x
        at_y = found[1] - mid_y
        con_a, con_b, con_c, opacity = found[2:6]
        line_x = -2.0 * con_a * at_x - con_b * at_y
        line_y = -2.0 * con_c * at_y - con_b * at_x
        level = opacity - 0.5 * (line_x * at_x + line_y * at_y)
        coefs = [jnp.where(keep, level, -30000.0)]
        coefs += [jnp.where(keep, row, 0.0) for row in (line_x, line_y, con_a, con_b, con_c)]
        for j in range(6):
            pieces = parts(coefs[j], 3)
            for step in range(3):
                coef_ref[6 * step + j : 6 * step + j + 1, :] = pieces[step].astype(jnp.float32)
        for k in range(3):
            coef_ref[18 + k : 19 + k, :] = found[6 + k]
        coef_ref[21:22, :] = index.astype(jnp.float32)
        for j, row in enumerate((at_x, at_y, con_a, con_b, con_c)):
            coef_ref[22 + j : 23 + j, :] = row
        first = pl.multiple_of(g * GROUP, GROUP)
        for c in range(GROUP // 128):
            plain_ref[128 * c : 128 * c + 128, :] = coef_ref[:, 128 * c : 128 * c + 128].T
        turned = jnp.concatenate([plain_ref[pl.ds(i, SEGS, stride=SEG), :] for i in range(SEG)], axis=0)
        wide_ref[pl.ds(first, GROUP), :] = turned
        tint_ref[...] = turned
        power = jnp.dot(turned.astype(jnp.bfloat16), basis_ref[...], preferred_element_type=jnp.float32)
        power_ref[...] = power

    def forward(g, power_ref, tint_ref):
        first = pl.multiple_of(g * GROUP, GROUP)
        zero = jnp.zeros((SEGS, 256), jnp.float32)
        transmit = jnp.ones((SEGS, 256), jnp.float32)
        lights = [zero, zero, zero]
        for i in range(SEG):
            alpha = jnp.exp2(power_ref[SEGS * i : SEGS * i + SEGS, :])
            weight = alpha * transmit
            transmit = transmit - weight
            alpha_ref[pl.ds(first + SEGS * i, SEGS), :] = alpha
            weight_ref[pl.ds(first + SEGS * i, SEGS), :] = weight
            tint = tint_ref[SEGS * i : SEGS * i + SEGS, :]
            lights = [lights[k] + weight * tint[:, 18 + k : 19 + k] for k in range(3)]
        for s in range(SEGS):
            n = SEGS * g + s
            spot = seg_place[n] * 16 + seg_tile[n]
            pass_ref[pl.ds(spot, 1), :] = transmit[s : s + 1]
            for k in range(3):
                light_ref[k, pl.ds(spot, 1), :] = lights[k][s : s + 1]

    buffers = ((power_a_ref, tint_a_ref), (power_b_ref, tint_b_ref))

    def forward_pair(p, carry):
        prepare(2 * p + 1, *buffers[1])
        forward(2 * p, *buffers[0])
        prepare(2 * p + 2, *buffers[0])
        forward(2 * p + 1, *buffers[1])
        return carry

    prepare(0, *buffers[0])
    lax.fori_loop(0, groups >> 1, forward_pair, 0)

    @pl.when((groups & 1) == 1)
    def _():
        forward(groups - 1, *buffers[0])

    transmit = jnp.ones((16, 256), jnp.float32)
    image = [jnp.zeros((16, 256), jnp.float32) for _ in range(3)]
    for place in range(16):
        span = slice(16 * place, 16 * place + 16)
        start_ref[span, :] = transmit
        image = [image[k] + transmit * light_ref[k, span, :] for k in range(3)]
        transmit = transmit * pass_ref[span, :]
    resid = []
    for k in range(3):
        image_ref[k] = image[k]
        resid.append(image[k] - target_ref[k])
        resid_ref[k] = resid[k]
    behind = jnp.zeros((16, 256), jnp.float32)
    for place in reversed(range(16)):
        span = slice(16 * place, 16 * place + 16)
        behind_ref[span, :] = behind
        own = sum(resid[k] * light_ref[k, span, :] for k in range(3))
        behind = own + pass_ref[span, :] * behind

    segment = lax.broadcasted_iota(jnp.int32, (SEGS, GROUP), 0)
    own_lane = segment == (lax.broadcasted_iota(jnp.int32, (SEGS, GROUP), 1) & (SEGS - 1))

    def rows_at(ref, places):
        return jnp.concatenate([ref[pl.ds(place, 1), :] for place in places], axis=0)

    def backward(g, pieces_ref):
        first = pl.multiple_of(g * GROUP, GROUP)
        tiles = [seg_tile[SEGS * g + s] for s in range(SEGS)]
        spots = [seg_place[SEGS * g + s] * 16 + tiles[s] for s in range(SEGS)]
        start = rows_at(start_ref, spots)
        behind = rows_at(behind_ref, spots)
        resid = [rows_at(resid_ref.at[k], tiles) for k in range(3)]
        for i in reversed(range(SEG)):
            here = first + SEGS * i
            tint = wide_ref[pl.ds(here, SEGS), :]
            shade = resid[0] * tint[:, 18:19] + resid[1] * tint[:, 19:20] + resid[2] * tint[:, 20:21]
            ahead = shade - behind
            behind = behind + alpha_ref[pl.ds(here, SEGS), :] * ahead
            weight = start * weight_ref[pl.ds(here, SEGS), :]
            for k, values in enumerate((weight * ahead, weight)):
                high, rest = parts(values, 2)
                pieces_ref[SEGS * i : SEGS * i + SEGS, 512 * k : 512 * k + 256] = high
                pieces_ref[SEGS * i : SEGS * i + SEGS, 512 * k + 256 : 512 * k + 512] = rest

    def across(left, right):
        return lax.dot_general(left, right, (((1,), (1,)), ((), ())), preferred_element_type=jnp.float32)

    def collect(g, pieces_ref):
        first = pl.multiple_of(g * GROUP, GROUP)
        wide = wide_ref[pl.ds(first, GROUP), :]
        known = jnp.concatenate([wide[128 * c : 128 * c + 128].T for c in range(GROUP // 128)], axis=1)
        tiles = [seg_tile[SEGS * g + s] for s in range(SEGS)]
        resid = [parts(rows_at(resid_ref.at[k], tiles), 2) for k in range(3)]
        resid = jnp.concatenate([resid[k][step] for step in range(2) for k in range(3)], axis=0)
        moments = across(moment_ref[...], pieces_ref[:, 0:512])
        light = across(jnp.concatenate([resid, resid], axis=1), pieces_ref[:, 512:1024])
        m_0, m_x, m_y, m_xx, m_xy, m_yy = [LN2 * moments[j : j + 1] for j in range(6)]
        at_x, at_y, con_a, con_b, con_c = [known[22 + j : 23 + j] for j in range(5)]
        s_x = m_x - at_x * m_0
        s_y = m_y - at_y * m_0
        s_xx = m_xx - at_x * (m_x + s_x)
        s_xy = m_xy - at_x * m_y - at_y * s_x
        s_yy = m_yy - at_y * (m_y + s_y)
        rows = [
            -(2.0 * con_a * s_x + con_b * s_y),
            -(2.0 * con_c * s_y + con_b * s_x),
            s_xx,
            s_xy,
            s_yy,
            m_0,
        ]
        for k in range(3):
            both = light[16 * k : 16 * k + 16] + light[48 + 16 * k : 64 + 16 * k]
            rows.append(jnp.sum(jnp.where(own_lane, both, 0.0), axis=0, keepdims=True))
        scatter_features(total_ref, rows, known[21:22].astype(jnp.int32), wide[:, 21:22])

    def backward_pair(p, carry):
        backward(2 * p + 1, pieces_b_ref)
        collect(2 * p, pieces_a_ref)
        backward(2 * p + 2, pieces_a_ref)
        collect(2 * p + 1, pieces_b_ref)
        return carry

    backward(0, pieces_a_ref)
    lax.fori_loop(0, groups >> 1, backward_pair, 0)

    @pl.when((groups & 1) == 1)
    def _():
        collect(groups - 1, pieces_a_ref)

    unpack_total(total_ref, table_ref)
    table_to_blocks(table_ref, send_ref)


def smem():
    return pl.BlockSpec(memory_space=pltpu.SMEM)


def vmem():
    return pl.BlockSpec(memory_space=pltpu.VMEM)


def limits(mib):
    return pltpu.CompilerParams(vmem_limit_bytes=mib * 1024 * 1024)


def run_project(camera, gaussians):
    return pl.pallas_call(
        project_kernel,
        out_shape=jax.ShapeDtypeStruct((ROWS, 256), jnp.bfloat16),
        in_specs=[smem(), vmem()],
        out_specs=vmem(),
        scratch_shapes=[pltpu.VMEM((4096, 128), jnp.float32), pltpu.VMEM((FEATS, 64, 128), jnp.float32)],
        compiler_params=limits(16),
        name="project",
    )(camera, gaussians)


def run_fetch(parity, packed, asked):
    return pl.pallas_call(
        fetch_kernel,
        out_shape=(
            jax.ShapeDtypeStruct((64, 128), jnp.int32),
            jax.ShapeDtypeStruct((640, 128), jnp.float32),
        ),
        in_specs=[smem(), vmem(), vmem()],
        out_specs=(vmem(), vmem()),
        scratch_shapes=[pltpu.VMEM((FEATS, 64, 128), jnp.float32)],
        compiler_params=limits(16),
        name="fetch",
    )(parity, packed, asked)


def run_plan(counts, active, after):
    segments = jax.ShapeDtypeStruct((SEGS * (MAX_GROUPS + 1),), jnp.int32)
    return pl.pallas_call(
        plan_kernel,
        out_shape=(segments, segments, jax.ShapeDtypeStruct((1,), jnp.int32)),
        in_specs=[smem(), smem(), pl.BlockSpec(memory_space=pl.ANY)],
        out_specs=(smem(), smem(), smem()),
        name="plan",
    )(counts, active, after)


def run_render(tile_ids, counts, segments, received, lists, target):
    f32, bf16 = jnp.float32, jnp.bfloat16
    entries = (MAX_GROUPS + 1) * GROUP
    return pl.pallas_call(
        render_kernel,
        out_shape=(
            jax.ShapeDtypeStruct((3, 16, 256), f32),
            jax.ShapeDtypeStruct((640, 128), f32),
        ),
        in_specs=[smem()] * 5 + [vmem()] * 3,
        out_specs=(vmem(), vmem()),
        scratch_shapes=[
            pltpu.VMEM((FEATS, 64, 128), f32),
            pltpu.VMEM((ROWS, 256), bf16),
            pltpu.VMEM((BACK_ROWS, 256), f32),
            pltpu.VMEM((32, 256), bf16),
            pltpu.VMEM((16, 512), bf16),
            pltpu.VMEM((32, GROUP), f32),
            pltpu.VMEM((GROUP, 32), f32),
            pltpu.VMEM((entries, 32), f32),
            pltpu.VMEM((GROUP, 256), f32),
            pltpu.VMEM((GROUP, 256), f32),
            pltpu.VMEM((GROUP, 32), f32),
            pltpu.VMEM((GROUP, 32), f32),
            pltpu.VMEM((entries, 256), f32),
            pltpu.VMEM((entries, 256), f32),
            pltpu.VMEM((272, 256), f32),
            pltpu.VMEM((3, 272, 256), f32),
            pltpu.VMEM((272, 256), f32),
            pltpu.VMEM((272, 256), f32),
            pltpu.VMEM((3, 16, 256), f32),
            pltpu.VMEM((GROUP, 1024), bf16),
            pltpu.VMEM((GROUP, 1024), bf16),
        ],
        compiler_params=limits(48),
        name="render",
    )(tile_ids, counts, *segments, received, lists, target)


def run_return(camera, gaussians, index, back):
    return pl.pallas_call(
        return_kernel,
        out_shape=jax.ShapeDtypeStruct((59, 8192), jnp.float32),
        in_specs=[smem(), vmem(), vmem(), vmem()],
        out_specs=vmem(),
        scratch_shapes=[
            pltpu.VMEM((4096, 128), jnp.float32),
            pltpu.VMEM((FEATS, 64, 128), jnp.float32),
            pltpu.VMEM((BACK_ROWS, 256), jnp.float32),
        ],
        compiler_params=limits(24),
        name="give_back",
    )(camera, gaussians, index, back)


def exchange(rows):
    count = rows.shape[0] // 128 * rows.shape[1]
    moved = lax.all_to_all(rows.reshape(128, 1, count), AXES, split_axis=0, concat_axis=0, tiled=True)
    return moved.reshape(rows.shape)


def local(gaussians, camera, asked, parity, tile_ids, tile_lists, tile_counts, tile_active, target, send_on):
    lists = tile_lists.reshape(128, 128)
    packed = run_project(camera, gaussians)
    index, send = run_fetch(parity, packed, asked)
    segments = run_plan(tile_counts, tile_active, index)
    image, back = run_render(tile_ids, tile_counts, segments, send_on(send), lists, target)
    grads = run_return(camera, gaussians, index, send_on(back))
    return (image, grads)


def per_device(gaussians, camera, fetch_index, tile_ids, tile_lists, tile_counts, tile_active, target):
    asked = exchange(jnp.repeat(fetch_index.reshape(64, 128), 2, axis=0))
    parity = (lax.axis_index("shard") % 2).astype(jnp.int32).reshape(1)
    return local(gaussians, camera, asked, parity, tile_ids, tile_lists, tile_counts, tile_active, target, exchange)


def solution(mesh):
    in_specs = (
        P(None, AXES),
        P(),
        P(AXES, None),
        P(AXES, None),
        P(AXES, None, None),
        P(AXES, None),
        P(AXES, None),
        P(None, AXES, None),
    )
    out_specs = (P(None, AXES, None), P(None, AXES))
    return jax.shard_map(per_device, mesh=mesh, in_specs=in_specs, out_specs=out_specs, check_vma=False)
```

```python
import functools

import jax
import jax.numpy as jnp
from jax import lax
from jax.experimental import pallas as pl
from jax.experimental.pallas import tpu as pltpu
from jax.sharding import PartitionSpec as P

AXES = ("tile", "shard")
SEG = 64
SEGS = 16
GROUP = SEG * SEGS
MAX_GROUPS = 9
LOG2E = 1.4426950408889634
LN2 = 0.6931471805599453
FEATS = 9
TRIPLE = (0, 1)
ROWS = 32 * (2 * FEATS + len(TRIPLE))
BACK_ROWS = 32 * 2 * FEATS

SH_ZERO = 0.28209479177387814
SH_ONE = 0.4886025119029199
SH_TWO = (
    1.0925484305920792,
    -1.0925484305920792,
    0.31539156525252005,
    -1.0925484305920792,
    0.5462742152960396,
)
SH_THREE = (
    -0.5900435899266435,
    2.890611442640554,
    -0.4570457994644658,
    0.3731763325901154,
    -0.4570457994644658,
    1.445305721320277,
    -0.5900435899266435,
)


def harmonics(dir_x, dir_y, dir_z):
    sq_x, sq_y, sq_z = (dir_x * dir_x, dir_y * dir_y, dir_z * dir_z)
    return [
        None,
        -SH_ONE * dir_y,
        SH_ONE * dir_z,
        -SH_ONE * dir_x,
        SH_TWO[0] * dir_x * dir_y,
        SH_TWO[1] * dir_y * dir_z,
        SH_TWO[2] * (2.0 * sq_z - sq_x - sq_y),
        SH_TWO[3] * dir_x * dir_z,
        SH_TWO[4] * (sq_x - sq_y),
        SH_THREE[0] * dir_y * (3.0 * sq_x - sq_y),
        SH_THREE[1] * dir_x * dir_y * dir_z,
        SH_THREE[2] * dir_y * (4.0 * sq_z - sq_x - sq_y),
        SH_THREE[3] * dir_z * (2.0 * sq_z - 3.0 * sq_x - 3.0 * sq_y),
        SH_THREE[4] * dir_x * (4.0 * sq_z - sq_x - sq_y),
        SH_THREE[5] * dir_z * (sq_x - sq_y),
        SH_THREE[6] * dir_x * (sq_x - 3.0 * sq_y),
    ]


def project(rows, camera):
    focal_x, focal_y, centre_x, centre_y = camera
    mean_x, mean_y, mean_z = rows[0:3]
    spread = [jnp.exp(row) for row in rows[3:6]]
    q_w, q_x, q_y, q_z = rows[6:10]
    scale = lax.rsqrt(q_w * q_w + q_x * q_x + q_y * q_y + q_z * q_z)
    w_part, x_part, y_part, z_part = (q_w * scale, q_x * scale, q_y * scale, q_z * scale)
    rotate = [
        [
            1.0 - 2.0 * (y_part * y_part + z_part * z_part),
            2.0 * (x_part * y_part - w_part * z_part),
            2.0 * (x_part * z_part + w_part * y_part),
        ],
        [
            2.0 * (x_part * y_part + w_part * z_part),
            1.0 - 2.0 * (x_part * x_part + z_part * z_part),
            2.0 * (y_part * z_part - w_part * x_part),
        ],
        [
            2.0 * (x_part * z_part - w_part * y_part),
            2.0 * (y_part * z_part + w_part * x_part),
            1.0 - 2.0 * (x_part * x_part + y_part * y_part),
        ],
    ]
    depth_inv = 1.0 / mean_z
    along_x = mean_x * depth_inv
    along_y = mean_y * depth_inv
    lens_x = focal_x * depth_inv
    lens_y = focal_y * depth_inv
    first = [lens_x * (rotate[0][c] - along_x * rotate[2][c]) * spread[c] for c in range(3)]
    second = [lens_y * (rotate[1][c] - along_y * rotate[2][c]) * spread[c] for c in range(3)]
    cov_a = first[0] * first[0] + first[1] * first[1] + first[2] * first[2] + 0.3
    cov_b = first[0] * second[0] + first[1] * second[1] + first[2] * second[2]
    cov_c = second[0] * second[0] + second[1] * second[1] + second[2] * second[2] + 0.3
    inverse = LOG2E / (cov_a * cov_c - cov_b * cov_b)
    conic_a = -0.5 * cov_c * inverse
    conic_b = cov_b * inverse
    conic_c = -0.5 * cov_a * inverse
    screen_x = focal_x * along_x + centre_x
    screen_y = focal_y * along_y + centre_y
    opacity = -LOG2E * jnp.log(1.0 + jnp.exp(-rows[10]))
    radius = lax.rsqrt(mean_x * mean_x + mean_y * mean_y + mean_z * mean_z)
    basis = harmonics(mean_x * radius, mean_y * radius, mean_z * radius)
    colours = []
    for k in range(3):
        total = SH_ZERO * rows[11 + 16 * k] + 0.5
        for j in range(1, 16):
            total = total + basis[j] * rows[11 + 16 * k + j]
        colours.append(jnp.maximum(total, 0.0))
    return [screen_x, screen_y, conic_a, conic_b, conic_c, opacity] + colours


def low_half(shape):
    return lax.broadcasted_iota(jnp.int32, shape, len(shape) - 1) < 64


def swap(values):
    return pltpu.roll(values, 64, axis=1)


def spread_tiles(gaussians_ref, flat_ref):
    def body(t, carry):
        lanes = pl.ds(pl.multiple_of(t * 128, 128), 128)
        for g in range(8):
            size = 8 if g < 7 else 3
            start = pl.multiple_of((g * 64 + t) * 8, 8)
            flat_ref[pl.ds(start, size), :] = gaussians_ref[8 * g : 8 * g + size, lanes]
        return carry

    lax.fori_loop(0, 64, body, 0, unroll=4)


def param_rows(flat_ref, chunk, size):
    return [
        flat_ref[pl.ds((k // 8) * 512 + k % 8 + chunk * size * 8, size, stride=8), :]
        for k in range(59)
    ]


def parts(values, count):
    out = []
    for step in range(count):
        piece = values.astype(jnp.bfloat16)
        out.append(piece)
        if step + 1 < count:
            values = values - piece.astype(jnp.float32)
    return out


def pack_table(table_ref, packed_ref):
    extra = 2 * FEATS
    for f in range(FEATS):
        whole = jnp.concatenate(
            [table_ref[f, pl.ds(0, 32, stride=2), :], table_ref[f, pl.ds(1, 32, stride=2), :]], axis=1
        )
        pieces = parts(whole, 3 if f in TRIPLE else 2)
        packed_ref[64 * f : 64 * f + 32, :] = pieces[0]
        packed_ref[64 * f + 32 : 64 * f + 64, :] = pieces[1]
        if f in TRIPLE:
            packed_ref[32 * extra : 32 * extra + 32, :] = pieces[2]
            extra += 1


def one_hot(index):
    count = index.shape[1]
    rows = lax.broadcasted_iota(jnp.int32, (256, count), 0)
    return jnp.where(rows == (index & 255), 1.0, 0.0).astype(jnp.bfloat16)


def upper_mask(index):
    count = index.shape[1]
    rows = lax.broadcasted_iota(jnp.int32, (32, count), 0)
    return jnp.where(rows == (index >> 8), 1.0, 0.0)


def gather_features(packed_ref, index):
    mask = upper_mask(index)
    found = jnp.dot(packed_ref[...], one_hot(index), preferred_element_type=jnp.float32)
    out = []
    extra = 2 * FEATS
    for f in range(FEATS):
        block = found[64 * f : 64 * f + 32] + found[64 * f + 32 : 64 * f + 64]
        if f in TRIPLE:
            block = block + found[32 * extra : 32 * extra + 32]
            extra += 1
        out.append(jnp.sum(block * mask, axis=0, keepdims=True))
    return out


def one_hot_rows(column):
    lanes = lax.broadcasted_iota(jnp.int32, (column.shape[0], 256), 1)
    return jnp.where(lanes == (column.astype(jnp.int32) & 255), 1.0, 0.0).astype(jnp.bfloat16)


def scatter_features(total_ref, rows, index, column):
    mask = upper_mask(index).astype(jnp.bfloat16)
    blocks = []
    for row in rows:
        for piece in parts(row, 2):
            blocks.append(mask * piece)
    total_ref[...] += jnp.dot(
        jnp.concatenate(blocks, axis=0), one_hot_rows(column), preferred_element_type=jnp.float32
    )


def unpack_total(total_ref, table_ref):
    for f in range(FEATS):
        whole = total_ref[64 * f : 64 * f + 32, :] + total_ref[64 * f + 32 : 64 * f + 64, :]
        table_ref[f, pl.ds(0, 32, stride=2), :] = whole[:, :128]
        table_ref[f, pl.ds(1, 32, stride=2), :] = whole[:, 128:]


def table_to_blocks(table_ref, out_ref):
    low = low_half((64, 128))
    for i in range(5):
        even = table_ref[2 * i]
        odd = table_ref[2 * i + 1] if 2 * i + 1 < FEATS else jnp.zeros((64, 128), jnp.float32)
        out_ref[pl.ds(i, 64, stride=10), :] = jnp.where(low, even, swap(odd))
        out_ref[pl.ds(5 + i, 64, stride=10), :] = jnp.where(low, swap(even), odd)


def blocks_to_table(in_ref, table_ref):
    low = low_half((64, 128))
    for i in range(5):
        first = in_ref[pl.ds(i, 64, stride=10), :]
        second = in_ref[pl.ds(5 + i, 64, stride=10), :]
        table_ref[2 * i] = jnp.where(low, first, swap(second))
        if 2 * i + 1 < FEATS:
            table_ref[2 * i + 1] = jnp.where(low, swap(first), second)


def row_of(ref, q):
    return jnp.concatenate([ref[pl.ds(4 * q + c, 1), :] for c in range(4)], axis=1)


CHUNK = 8


def project_kernel(camera_ref, gaussians_ref, packed_ref, flat_ref, table_ref):
    camera = [camera_ref[k] for k in range(4)]
    spread_tiles(gaussians_ref, flat_ref)

    def body(chunk, carry):
        features = project(param_rows(flat_ref, chunk, CHUNK), camera)
        for f in range(FEATS):
            table_ref[f, pl.ds(pl.multiple_of(chunk * CHUNK, CHUNK), CHUNK), :] = features[f]
        return carry

    lax.fori_loop(0, 64 // CHUNK, body, 0)
    pack_table(table_ref, packed_ref)


def plan_segments(counts_ref, active_ref):
    slot = lax.broadcasted_iota(jnp.int32, (1, 256), 1)
    end = jnp.int32(0)
    tile = jnp.zeros((1, 256), jnp.int32)
    first = jnp.zeros((1, 256), jnp.int32)
    for t in range(16):
        used = jnp.where(active_ref[0, t] > 0, (counts_ref[0, t] + (SEG - 1)) >> 6, 0)
        end = end + used
        past = slot >= end
        tile = tile + jnp.where(past, 1, 0)
        first = first + jnp.where(past, used, 0)
    spare = slot >= end
    tile = jnp.where(spare, 0, tile)
    place = jnp.where(spare, 16, slot - first)
    groups = jnp.zeros((1, 256), jnp.int32) + ((end + (SEGS - 1)) >> 4)
    return jnp.concatenate([tile, place, groups, groups], axis=0)


def fetch_kernel(
    parity_ref, counts_ref, active_ref, packed_ref, asked_ref, index_ref, send_ref, plan_ref, table_ref
):
    plan_ref[...] = plan_segments(counts_ref, active_ref)
    low = low_half((64, 128))
    even = asked_ref[pl.ds(0, 64, stride=2), :]
    odd = asked_ref[pl.ds(1, 64, stride=2), :]
    index_ref[...] = jnp.where(
        parity_ref[0] == 0,
        jnp.where(low, even, swap(odd)),
        jnp.where(low, swap(even), odd),
    )

    for q in range(16):
        rows = gather_features(packed_ref, row_of(index_ref, q))
        for f in range(FEATS):
            for c in range(4):
                table_ref[f, 4 * q + c : 4 * q + c + 1, :] = rows[f][:, 128 * c : 128 * c + 128]
    table_to_blocks(table_ref, send_ref)


def return_kernel(camera_ref, gaussians_ref, index_ref, back_ref, grads_ref, flat_ref, table_ref, total_ref):
    camera = [camera_ref[k] for k in range(4)]
    spread_tiles(gaussians_ref, flat_ref)
    blocks_to_table(back_ref, table_ref)
    total_ref[...] = jnp.zeros_like(total_ref)
    columns = jnp.concatenate([index_ref[...].astype(jnp.float32), jnp.zeros((64, 128), jnp.float32)], axis=0).T
    for q in range(16):
        rows = [row_of(table_ref.at[f], q) for f in range(FEATS)]
        column = jnp.concatenate([columns[:, 4 * q + c : 4 * q + c + 1] for c in range(4)], axis=0)
        scatter_features(total_ref, rows, row_of(index_ref, q), column)
    unpack_total(total_ref, table_ref)

    def body(chunk, carry):
        params = param_rows(flat_ref, chunk, CHUNK)
        _, pullback = jax.vjp(lambda rows: project(rows, camera), params)
        place = pl.ds(pl.multiple_of(chunk * CHUNK, CHUNK), CHUNK)
        (grads,) = pullback([table_ref[f, place, :] for f in range(FEATS)])
        for k in range(59):
            start = (k // 8) * 512 + k % 8 + chunk * CHUNK * 8
            flat_ref[pl.ds(start, CHUNK, stride=8), :] = grads[k]
        return carry

    lax.fori_loop(0, 64 // CHUNK, body, 0)

    def out(t, carry):
        lanes = pl.ds(pl.multiple_of(t * 128, 128), 128)
        for g in range(8):
            size = 8 if g < 7 else 3
            start = pl.multiple_of((g * 64 + t) * 8, 8)
            grads_ref[8 * g : 8 * g + size, lanes] = flat_ref[pl.ds(start, size), :]
        return carry

    lax.fori_loop(0, 64, out, 0, unroll=4)


def monomials():
    lane = lax.broadcasted_iota(jnp.int32, (1, 256), 1)
    x = (lane & 15).astype(jnp.float32) - 7.5
    y = (lane >> 4).astype(jnp.float32) - 7.5
    return [jnp.ones((1, 256), jnp.float32), x, y, x * x, x * y, y * y]


def render_kernel(
    ids_ref,
    counts_ref,
    plan_ref,
    recv_ref,
    lists_ref,
    target_ref,
    image_ref,
    send_ref,
    table_ref,
    packed_ref,
    total_ref,
    basis_ref,
    moment_ref,
    coef_ref,
    plain_ref,
    wide_ref,
    power_a_ref,
    power_b_ref,
    tint_a_ref,
    tint_b_ref,
    alpha_ref,
    weight_ref,
    pass_ref,
    light_ref,
    start_ref,
    behind_ref,
    resid_ref,
    pieces_a_ref,
    pieces_b_ref,
):
    groups = plan_ref[2, 0]
    blocks_to_table(recv_ref, table_ref)
    pack_table(table_ref, packed_ref)
    total_ref[...] = jnp.zeros_like(total_ref)
    pass_ref[...] = jnp.ones_like(pass_ref)
    light_ref[...] = jnp.zeros_like(light_ref)
    coef_ref[...] = jnp.zeros_like(coef_ref)
    start_ref[256:272, :] = jnp.zeros((16, 256), jnp.float32)
    behind_ref[256:272, :] = jnp.zeros((16, 256), jnp.float32)
    terms = monomials()
    basis_rows = terms * 3 + [jnp.zeros((1, 256), jnp.float32)] * 14
    basis_ref[...] = jnp.concatenate(basis_rows, axis=0).astype(jnp.bfloat16)
    flat = jnp.concatenate(terms + [jnp.zeros((1, 256), jnp.float32)] * 10, axis=0)
    moment_ref[...] = jnp.concatenate([flat, flat], axis=1).astype(jnp.bfloat16)

    low = low_half((1, 128))
    lane = lax.broadcasted_iota(jnp.int32, (1, 128), 1) & 63

    def prepare(g, power_ref, tint_ref):
        index, keep, mid_x, mid_y = [], [], [], []
        for c in range(SEGS // 2):
            pair = []
            for half in range(2):
                n = SEGS * g + 2 * c + half
                t, place = plan_ref[0, n], plan_ref[1, n]
                near = jnp.minimum(place, 15)
                row = lists_ref[pl.ds(t * 8 + (near >> 1), 1), :]
                row = jnp.where((near & 1) == half, row, swap(row))
                screen = ids_ref[0, t]
                pair.append(
                    (
                        row,
                        counts_ref[0, t] - place * SEG,
                        ((screen & 63) * 16 + 8).astype(jnp.float32),
                        ((screen >> 6) * 16 + 8).astype(jnp.float32),
                    )
                )
            index.append(jnp.where(low, pair[0][0], pair[1][0]))
            keep.append(lane < jnp.where(low, pair[0][1], pair[1][1]))
            mid_x.append(jnp.where(low, pair[0][2], pair[1][2]))
            mid_y.append(jnp.where(low, pair[0][3], pair[1][3]))
        index = jnp.concatenate(index, axis=1)
        keep = jnp.concatenate([jnp.where(part, 1.0, 0.0) for part in keep], axis=1) > 0.5
        mid_x = jnp.concatenate(mid_x, axis=1)
        mid_y = jnp.concatenate(mid_y, axis=1)
        found = gather_features(packed_ref, index)
        at_x = found[0] - mid_x
        at_y = found[1] - mid_y
        con_a, con_b, con_c, opacity = found[2:6]
        line_x = -2.0 * con_a * at_x - con_b * at_y
        line_y = -2.0 * con_c * at_y - con_b * at_x
        level = opacity - 0.5 * (line_x * at_x + line_y * at_y)
        coefs = [jnp.where(keep, level, -30000.0)]
        coefs += [jnp.where(keep, row, 0.0) for row in (line_x, line_y, con_a, con_b, con_c)]
        for j in range(6):
            pieces = parts(coefs[j], 3)
            for step in range(3):
                coef_ref[6 * step + j : 6 * step + j + 1, :] = pieces[step].astype(jnp.float32)
        for k in range(3):
            coef_ref[18 + k : 19 + k, :] = found[6 + k]
        coef_ref[21:22, :] = index.astype(jnp.float32)
        for j, row in enumerate((at_x, at_y, con_a, con_b, con_c)):
            coef_ref[22 + j : 23 + j, :] = row
        first = pl.multiple_of(g * GROUP, GROUP)
        for c in range(GROUP // 128):
            plain_ref[128 * c : 128 * c + 128, :] = coef_ref[:, 128 * c : 128 * c + 128].T
        turned = jnp.concatenate([plain_ref[pl.ds(i, SEGS, stride=SEG), :] for i in range(SEG)], axis=0)
        wide_ref[pl.ds(first, GROUP), :] = turned
        tint_ref[...] = turned
        power = jnp.dot(turned.astype(jnp.bfloat16), basis_ref[...], preferred_element_type=jnp.float32)
        power_ref[...] = power

    def forward(g, power_ref, tint_ref):
        first = pl.multiple_of(g * GROUP, GROUP)
        zero = jnp.zeros((SEGS, 256), jnp.float32)
        transmit = jnp.ones((SEGS, 256), jnp.float32)
        lights = [zero, zero, zero]
        for i in range(SEG):
            alpha = jnp.exp2(power_ref[SEGS * i : SEGS * i + SEGS, :])
            weight = alpha * transmit
            transmit = transmit - weight
            alpha_ref[pl.ds(first + SEGS * i, SEGS), :] = alpha
            weight_ref[pl.ds(first + SEGS * i, SEGS), :] = weight
            tint = tint_ref[SEGS * i : SEGS * i + SEGS, :]
            lights = [lights[k] + weight * tint[:, 18 + k : 19 + k] for k in range(3)]
        for s in range(SEGS):
            n = SEGS * g + s
            spot = plan_ref[1, n] * 16 + plan_ref[0, n]
            pass_ref[pl.ds(spot, 1), :] = transmit[s : s + 1]
            for k in range(3):
                light_ref[k, pl.ds(spot, 1), :] = lights[k][s : s + 1]

    buffers = ((power_a_ref, tint_a_ref), (power_b_ref, tint_b_ref))

    def forward_pair(p, carry):
        prepare(2 * p + 1, *buffers[1])
        forward(2 * p, *buffers[0])
        prepare(2 * p + 2, *buffers[0])
        forward(2 * p + 1, *buffers[1])
        return carry

    prepare(0, *buffers[0])
    lax.fori_loop(0, groups >> 1, forward_pair, 0)

    @pl.when((groups & 1) == 1)
    def _():
        forward(groups - 1, *buffers[0])

    transmit = jnp.ones((16, 256), jnp.float32)
    image = [jnp.zeros((16, 256), jnp.float32) for _ in range(3)]
    for place in range(16):
        span = slice(16 * place, 16 * place + 16)
        start_ref[span, :] = transmit
        image = [image[k] + transmit * light_ref[k, span, :] for k in range(3)]
        transmit = transmit * pass_ref[span, :]
    resid = []
    for k in range(3):
        image_ref[k] = image[k]
        resid.append(image[k] - target_ref[k])
        resid_ref[k] = resid[k]
    behind = jnp.zeros((16, 256), jnp.float32)
    for place in reversed(range(16)):
        span = slice(16 * place, 16 * place + 16)
        behind_ref[span, :] = behind
        own = sum(resid[k] * light_ref[k, span, :] for k in range(3))
        behind = own + pass_ref[span, :] * behind

    segment = lax.broadcasted_iota(jnp.int32, (SEGS, GROUP), 0)
    own_lane = segment == (lax.broadcasted_iota(jnp.int32, (SEGS, GROUP), 1) & (SEGS - 1))

    def rows_at(ref, places):
        return jnp.concatenate([ref[pl.ds(place, 1), :] for place in places], axis=0)

    def backward(g, pieces_ref):
        first = pl.multiple_of(g * GROUP, GROUP)
        tiles = [plan_ref[0, SEGS * g + s] for s in range(SEGS)]
        spots = [plan_ref[1, SEGS * g + s] * 16 + tiles[s] for s in range(SEGS)]
        start = rows_at(start_ref, spots)
        behind = rows_at(behind_ref, spots)
        resid = [rows_at(resid_ref.at[k], tiles) for k in range(3)]
        for i in reversed(range(SEG)):
            here = first + SEGS * i
            tint = wide_ref[pl.ds(here, SEGS), :]
            shade = resid[0] * tint[:, 18:19] + resid[1] * tint[:, 19:20] + resid[2] * tint[:, 20:21]
            ahead = shade - behind
            behind = behind + alpha_ref[pl.ds(here, SEGS), :] * ahead
            weight = start * weight_ref[pl.ds(here, SEGS), :]
            for k, values in enumerate((weight * ahead, weight)):
                high, rest = parts(values, 2)
                pieces_ref[SEGS * i : SEGS * i + SEGS, 512 * k : 512 * k + 256] = high
                pieces_ref[SEGS * i : SEGS * i + SEGS, 512 * k + 256 : 512 * k + 512] = rest

    def across(left, right):
        return lax.dot_general(left, right, (((1,), (1,)), ((), ())), preferred_element_type=jnp.float32)

    def collect(g, pieces_ref):
        first = pl.multiple_of(g * GROUP, GROUP)
        wide = wide_ref[pl.ds(first, GROUP), :]
        known = jnp.concatenate([wide[128 * c : 128 * c + 128].T for c in range(GROUP // 128)], axis=1)
        tiles = [plan_ref[0, SEGS * g + s] for s in range(SEGS)]
        resid = [parts(rows_at(resid_ref.at[k], tiles), 2) for k in range(3)]
        resid = jnp.concatenate([resid[k][step] for step in range(2) for k in range(3)], axis=0)
        moments = across(moment_ref[...], pieces_ref[:, 0:512])
        light = across(jnp.concatenate([resid, resid], axis=1), pieces_ref[:, 512:1024])
        m_0, m_x, m_y, m_xx, m_xy, m_yy = [LN2 * moments[j : j + 1] for j in range(6)]
        at_x, at_y, con_a, con_b, con_c = [known[22 + j : 23 + j] for j in range(5)]
        s_x = m_x - at_x * m_0
        s_y = m_y - at_y * m_0
        s_xx = m_xx - at_x * (m_x + s_x)
        s_xy = m_xy - at_x * m_y - at_y * s_x
        s_yy = m_yy - at_y * (m_y + s_y)
        rows = [
            -(2.0 * con_a * s_x + con_b * s_y),
            -(2.0 * con_c * s_y + con_b * s_x),
            s_xx,
            s_xy,
            s_yy,
            m_0,
        ]
        for k in range(3):
            both = light[16 * k : 16 * k + 16] + light[48 + 16 * k : 64 + 16 * k]
            rows.append(jnp.sum(jnp.where(own_lane, both, 0.0), axis=0, keepdims=True))
        scatter_features(total_ref, rows, known[21:22].astype(jnp.int32), wide[:, 21:22])

    def backward_pair(p, carry):
        backward(2 * p + 1, pieces_b_ref)
        collect(2 * p, pieces_a_ref)
        backward(2 * p + 2, pieces_a_ref)
        collect(2 * p + 1, pieces_b_ref)
        return carry

    backward(0, pieces_a_ref)
    lax.fori_loop(0, groups >> 1, backward_pair, 0)

    @pl.when((groups & 1) == 1)
    def _():
        collect(groups - 1, pieces_a_ref)

    unpack_total(total_ref, table_ref)
    table_to_blocks(table_ref, send_ref)


def smem():
    return pl.BlockSpec(memory_space=pltpu.SMEM)


def vmem():
    return pl.BlockSpec(memory_space=pltpu.VMEM)


def limits(mib):
    return pltpu.CompilerParams(vmem_limit_bytes=mib * 1024 * 1024)


def run_project(camera, gaussians):
    return pl.pallas_call(
        project_kernel,
        out_shape=jax.ShapeDtypeStruct((ROWS, 256), jnp.bfloat16),
        in_specs=[smem(), vmem()],
        out_specs=vmem(),
        scratch_shapes=[pltpu.VMEM((4096, 128), jnp.float32), pltpu.VMEM((FEATS, 64, 128), jnp.float32)],
        compiler_params=limits(16),
        name="project",
    )(camera, gaussians)


def run_fetch(parity, counts, active, packed, asked):
    return pl.pallas_call(
        fetch_kernel,
        out_shape=(
            jax.ShapeDtypeStruct((64, 128), jnp.int32),
            jax.ShapeDtypeStruct((640, 128), jnp.float32),
            jax.ShapeDtypeStruct((4, 256), jnp.int32),
        ),
        in_specs=[smem(), smem(), smem(), vmem(), vmem()],
        out_specs=(vmem(), vmem(), vmem()),
        scratch_shapes=[pltpu.VMEM((FEATS, 64, 128), jnp.float32)],
        compiler_params=limits(16),
        name="fetch",
    )(parity, counts, active, packed, asked)


def run_render(tile_ids, counts, plan, received, lists, target):
    f32, bf16 = jnp.float32, jnp.bfloat16
    entries = (MAX_GROUPS + 1) * GROUP
    return pl.pallas_call(
        render_kernel,
        out_shape=(
            jax.ShapeDtypeStruct((3, 16, 256), f32),
            jax.ShapeDtypeStruct((640, 128), f32),
        ),
        in_specs=[smem()] * 3 + [vmem()] * 3,
        out_specs=(vmem(), vmem()),
        scratch_shapes=[
            pltpu.VMEM((FEATS, 64, 128), f32),
            pltpu.VMEM((ROWS, 256), bf16),
            pltpu.VMEM((BACK_ROWS, 256), f32),
            pltpu.VMEM((32, 256), bf16),
            pltpu.VMEM((16, 512), bf16),
            pltpu.VMEM((32, GROUP), f32),
            pltpu.VMEM((GROUP, 32), f32),
            pltpu.VMEM((entries, 32), f32),
            pltpu.VMEM((GROUP, 256), f32),
            pltpu.VMEM((GROUP, 256), f32),
            pltpu.VMEM((GROUP, 32), f32),
            pltpu.VMEM((GROUP, 32), f32),
            pltpu.VMEM((entries, 256), f32),
            pltpu.VMEM((entries, 256), f32),
            pltpu.VMEM((272, 256), f32),
            pltpu.VMEM((3, 272, 256), f32),
            pltpu.VMEM((272, 256), f32),
            pltpu.VMEM((272, 256), f32),
            pltpu.VMEM((3, 16, 256), f32),
            pltpu.VMEM((GROUP, 1024), bf16),
            pltpu.VMEM((GROUP, 1024), bf16),
        ],
        compiler_params=limits(48),
        name="render",
    )(tile_ids, counts, plan, received, lists, target)


def run_return(camera, gaussians, index, back):
    return pl.pallas_call(
        return_kernel,
        out_shape=jax.ShapeDtypeStruct((59, 8192), jnp.float32),
        in_specs=[smem(), vmem(), vmem(), vmem()],
        out_specs=vmem(),
        scratch_shapes=[
            pltpu.VMEM((4096, 128), jnp.float32),
            pltpu.VMEM((FEATS, 64, 128), jnp.float32),
            pltpu.VMEM((BACK_ROWS, 256), jnp.float32),
        ],
        compiler_params=limits(24),
        name="give_back",
    )(camera, gaussians, index, back)


def exchange(rows):
    count = rows.shape[0] // 128 * rows.shape[1]
    moved = lax.all_to_all(rows.reshape(128, 1, count), AXES, split_axis=0, concat_axis=0, tiled=True)
    return moved.reshape(rows.shape)


def local(gaussians, camera, asked, parity, tile_ids, tile_lists, tile_counts, tile_active, target, send_on):
    lists = tile_lists.reshape(128, 128)
    packed = run_project(camera, gaussians)
    index, send, plan = run_fetch(parity, tile_counts, tile_active, packed, asked)
    image, back = run_render(tile_ids, tile_counts, plan, send_on(send), lists, target)
    grads = run_return(camera, gaussians, index, send_on(back))
    return (image, grads)


def per_device(gaussians, camera, fetch_index, tile_ids, tile_lists, tile_counts, tile_active, target):
    asked = exchange(jnp.repeat(fetch_index.reshape(64, 128), 2, axis=0))
    parity = (lax.axis_index("shard") % 2).astype(jnp.int32).reshape(1)
    return local(gaussians, camera, asked, parity, tile_ids, tile_lists, tile_counts, tile_active, target, exchange)


def solution(mesh):
    in_specs = (
        P(None, AXES),
        P(),
        P(AXES, None),
        P(AXES, None),
        P(AXES, None, None),
        P(AXES, None),
        P(AXES, None),
        P(None, AXES, None),
    )
    out_specs = (P(None, AXES, None), P(None, AXES))
    return jax.shard_map(per_device, mesh=mesh, in_specs=in_specs, out_specs=out_specs, check_vma=False)
```
